128 devices in a mesh: fluid: 16 (over z, x_hi, core), struct: 8 (over y, x_lo).
Axes of the slice: x: 4 (x_hi: 2, x_lo: 2; x = x_hi * 2 + x_lo), y: 4, z: 4, core: 2. Of those that a mesh axis runs over, the one named last changes fastest.
Arguments:
- fluid_adjoint: float32 [5, 65536], P(None, ('fluid', 'struct')), may hold values from -6 to 6
- fluid_rhs: float32 [5, 65536], P(None, ('fluid', 'struct')), may hold values from -6 to 6
- diag_inverse: float32 [5, 5, 65536], P(None, None, ('fluid', 'struct'))
- face_blocks: float32 [6, 5, 5, 65536], P(None, None, None, ('fluid', 'struct')), may hold values from -0.625 to 0.625
- face_index: int32 [6, 65536], P(None, ('fluid', 'struct')), may hold values from 0 to 1023, as said below
- surface_cell: int32 [32768], P(('fluid', 'struct')), may hold values from 0 to 511, as said below
- surface_count: int32 [128], P(('fluid', 'struct')), may hold values from 32 to 256, as said below
- transfer_node: int32 [3, 32768], P(None, ('fluid', 'struct')), may hold values from 0 to 4095
- transfer_weight: float32 [3, 32768], P(None, ('fluid', 'struct')), may hold values from 0.2 to 1
- load_sens: float32 [3, 5, 32768], P(None, None, ('fluid', 'struct')), may hold values from -4 to 4
- disp_sens: float32 [5, 3, 32768], P(None, None, ('fluid', 'struct')), may hold values from -2.4 to 2.4
- struct_adjoint: float32 [24576], P('struct'), may hold values from -6 to 6
- struct_rhs: float32 [24576], P('struct'), may hold values from -6 to 6
- shell_blocks: float32 [4, 256, 9216], P(None, 'struct'), may hold values from -0.15625 to 0.15625
- shell_inverse: float32 [256, 9216], P('struct')
- shell_columns: int32 [4, 256], P(None, 'struct'), may hold values from 0 to 255
Outputs:
- fluid_out: float32 [5, 65536], P(None, ('fluid', 'struct'))
- struct_out: float32 [24576], P('struct')
The draws below stay inside these ranges and needn't reach their ends.
Inputs may be any that keep to these rules, and one draw needn't show every extreme that they name: `face_index`: neighbour positions lie within 256 cells of the cell's own position in the extended block; the two ends of the range are taken. `surface_cell`: distinct within each block of 256 slots; every block holds the first and the last cell of the block. `surface_count`: some block has all its slots live and some has 32.
All inputs are finite; a program needn't handle non-finite values.
Results may differ from the reference program's by a relative error of at most 0.00021.
Values sent between devices are 32-bit elements; how exact they have to be, the bound alone decides.
No kernel may reach another device: no remote copies, remote signals or barrier semaphores. Data moves between devices by JAX's collectives and lax.ppermute only.
A program may use at most 64 MiB of HBM per device.

```python
import math
import jax
import jax.numpy as jnp
from jax import lax

NVAR = 5
FACES = 6
CELL_DEV = 512
HALO = 256
BLOCKS = 128
CELLS = 65536
SURF_DEV = 256
SURFS = 32768
TMAP = 3
DOF = 6
BLK = 96
NSB = 256
NODES = 4096
NB = 4
SWEEPS = 6
ITERS = 2


def draw_diag_inverse(key, part):
    first, second = jax.random.split(key)
    rows = jnp.arange(NVAR, dtype=jnp.int32)
    identity = (rows[:, None] == rows[None, :]).astype(jnp.float32)[:, :, None]
    scale = jnp.exp(jax.random.uniform(first, (1, 1, CELLS), jnp.float32, math.log(0.5), math.log(2.0)))
    spread = 0.25 * jax.random.normal(second, (NVAR, NVAR, CELLS), jnp.float32)
    return identity * scale + (1.0 - identity) * spread * scale


def draw_shell_inverse(key, part):
    first, second = jax.random.split(key)
    flat = jnp.arange(BLK * BLK, dtype=jnp.int32)
    identity = (flat // BLK == flat % BLK).astype(jnp.float32)[None, :]
    scale = jnp.exp(jax.random.uniform(first, (NSB, BLK * BLK), jnp.float32, math.log(0.5), math.log(2.0)))
    spread = 0.3 * BLK ** (-0.5) * jax.random.normal(second, (NSB, BLK * BLK), jnp.float32)
    return identity * scale + (1.0 - identity) * spread


def draw_face_index(key, part):
    position = jnp.arange(CELLS, dtype=jnp.int32) % CELL_DEV
    offsets = jax.random.randint(key, (FACES, CELLS), -HALO, HALO + 1, jnp.int32)
    faces = jnp.arange(FACES, dtype=jnp.int32)[:, None]
    offsets = jnp.where(faces == 0, -1, offsets)
    offsets = jnp.where(faces == 1, 1, offsets)
    offsets = jnp.where((faces == 2) & (position[None, :] == 0), -HALO, offsets)
    offsets = jnp.where((faces == FACES - 1) & (position[None, :] == CELL_DEV - 1), HALO, offsets)
    return (position[None, :] + HALO + offsets).astype(jnp.int32)


def pick_cells(single):
    first, second = jax.random.split(single)
    inner = jax.random.permutation(first, CELL_DEV - 2)[:SURF_DEV - 2].astype(jnp.int32) + 1
    ends = jnp.array([0, CELL_DEV - 1], jnp.int32)
    gathered = jnp.concatenate([ends, inner]).astype(jnp.int32)
    order = jax.random.permutation(second, SURF_DEV)
    return gathered[order]


def draw_surface_cell(key, part):
    keys = jax.random.split(key, BLOCKS)
    picked = jax.vmap(pick_cells)(keys)
    return picked.reshape(-1).astype(jnp.int32)


def draw_surface_count(key, part):
    first, second = jax.random.split(key)
    levels = SURF_DEV // jnp.array([1, 2, 4, 8], jnp.int32)
    counts = levels[jax.random.randint(first, (BLOCKS,), 0, 4, jnp.int32)]
    fullest = jax.random.randint(second, (), 0, BLOCKS, jnp.int32)
    blocks = jnp.arange(BLOCKS, dtype=jnp.int32)
    counts = jnp.where(blocks == fullest, SURF_DEV, counts)
    counts = jnp.where(blocks == (fullest + 1) % BLOCKS, SURF_DEV // 8, counts)
    return counts.astype(jnp.int32)


def set_ends(entries, stream_key, low, high):
    place = [jax.random.randint(jax.random.fold_in(stream_key, axis), (), 0, length) for axis, length in enumerate(entries.shape)]
    main_axis = entries.shape.index(max(entries.shape))
    beside = place[:main_axis] + [(place[main_axis] + 1) % entries.shape[main_axis]] + place[main_axis + 1:]
    return entries.at[tuple(place)].set(low).at[tuple(beside)].set(high)


def block_levels(key, shape, shards, smallest, high):
    gain = 1.0
    for dim, shards_of in shards:
        draws = jax.random.uniform(jax.random.fold_in(jax.random.fold_in(key, 6), dim), (shards_of,), jnp.float32, smallest / len(shards), high / len(shards))
        gain = gain * jnp.repeat(jnp.exp(draws), shape[dim] // shards_of).reshape((-1,) + (1,) * (len(shape) - 1 - dim))
    return gain


def noise(rng, shape, scale, reach, cuts=(), held_as=jnp.bfloat16):
    level = block_levels(rng, shape, cuts, -0.22, 0.18) if cuts else 1.0
    values = jax.random.normal(rng, shape, jnp.float32) * scale * level
    return jnp.minimum(jnp.maximum(values, -reach), reach).astype(held_as)


def setup_inputs(seed: int = 0) -> dict:
    key_of = jax.random.split(jax.random.key(seed), 17)
    return {
        "fluid_adjoint": noise(key_of[0], (NVAR, CELLS), 1.0, 6.0, ((1, 128),), jnp.float32),
        "fluid_rhs": noise(key_of[1], (NVAR, CELLS), 1.0, 6.0, ((1, 128),), jnp.float32),
        "diag_inverse": draw_diag_inverse(jax.random.fold_in(key_of[16], 71), 0),
        "face_blocks": noise(key_of[3], (FACES, NVAR, NVAR, CELLS), 100 ** -0.5, 0.625, ((3, 128),), jnp.float32),
        "face_index": draw_face_index(jax.random.fold_in(key_of[16], 71), 0),
        "surface_cell": draw_surface_cell(jax.random.fold_in(key_of[16], 71), 0),
        "surface_count": draw_surface_count(jax.random.fold_in(key_of[16], 71), 0),
        "transfer_node": set_ends(jax.random.randint(key_of[7], (TMAP, SURFS), 0, NODES), jax.random.fold_in(key_of[7], 1), 0, NODES - 1).astype(jnp.int32),
        "transfer_weight": jnp.clip(0.2 + 0.8 * jax.random.uniform(key_of[8], (TMAP, SURFS), jnp.float32) ** block_levels(key_of[8], (TMAP, SURFS), ((1, 128),), -0.2, 0.2), 0.2, 1.0),
        "load_sens": noise(key_of[9], (3, NVAR, SURFS), 0.5, 4.0, ((2, 128),), jnp.float32),
        "disp_sens": noise(key_of[10], (NVAR, 3, SURFS), 0.3, 2.4, ((2, 128),), jnp.float32),
        "struct_adjoint": noise(key_of[11], (NSB * BLK,), 1.0, 6.0, ((0, 8),), jnp.float32),
        "struct_rhs": noise(key_of[12], (NSB * BLK,), 1.0, 6.0, ((0, 8),), jnp.float32),
        "shell_blocks": noise(key_of[13], (NB, NSB, BLK * BLK), (4 * NB * BLK) ** -0.5, 0.15625, ((1, 8),), jnp.float32),
        "shell_inverse": draw_shell_inverse(jax.random.fold_in(key_of[16], 71), 0),
        "shell_columns": set_ends(jax.random.randint(key_of[15], (NB, NSB), 0, NSB), jax.random.fold_in(key_of[15], 1), 0, NSB - 1).astype(jnp.int32),
    }


def reference(fluid_adjoint, fluid_rhs, diag_inverse, face_blocks, face_index, surface_cell, surface_count, transfer_node, transfer_weight, load_sens, disp_sens, struct_adjoint, struct_rhs, shell_blocks, shell_inverse, shell_columns):
    highest = lax.Precision.HIGHEST
    cell_total = fluid_adjoint.shape[1]
    block_of_cell = (jnp.arange(cell_total, dtype=jnp.int32) // CELL_DEV).astype(jnp.int32)
    padded_index = (face_index + (block_of_cell * CELL_DEV)[None, :]).astype(jnp.int32)
    surf_total = surface_cell.shape[0]
    slot_ids = jnp.arange(surf_total, dtype=jnp.int32)
    surf_block = (slot_ids // SURF_DEV).astype(jnp.int32)
    global_cell = (surface_cell + surf_block * CELL_DEV).astype(jnp.int32)
    live_slot = (slot_ids % SURF_DEV < surface_count[surf_block]).astype(jnp.float32)
    component = jnp.arange(3, dtype=jnp.int32)
    dof_index = (transfer_node[:, None, :] * DOF + component[None, :, None]).astype(jnp.int32)
    fluid_state = fluid_adjoint
    struct_state = struct_adjoint
    for iteration in range(ITERS):
        displaced = jnp.sum(transfer_weight[:, None, :] * struct_state[dof_index], axis=0)
        load_adj = live_slot[None, :] * jnp.einsum("jvs,js->vs", load_sens, displaced, precision=highest)
        coupling = jnp.zeros_like(fluid_state).at[:, global_cell].add(load_adj)
        shell_rows = struct_state.reshape(NSB, BLK)[shell_columns]
        shell_terms = jnp.einsum("mbqp,mbq->bp", shell_blocks.reshape(NB, NSB, BLK, BLK), shell_rows, precision=highest)
        for sweep_step in range(SWEEPS):
            padded = jnp.pad(fluid_state, ((0, 0), (HALO, HALO)))
            beside = padded[:, padded_index]
            face_terms = jnp.einsum("kuvc,ukc->vc", face_blocks, beside, precision=highest)
            fluid_state = jnp.einsum("vuc,uc->vc", diag_inverse, fluid_rhs + coupling - face_terms, precision=highest)
        surface_sens = live_slot[None, :] * jnp.einsum("vjs,vs->js", disp_sens, fluid_state[:, global_cell], precision=highest)
        forces = jnp.zeros_like(struct_state).at[dof_index].add(transfer_weight[:, None, :] * surface_sens[None, :, :])
        struct_total = struct_rhs.reshape(NSB, BLK) + forces.reshape(NSB, BLK) - shell_terms
        struct_state = jnp.einsum("bpq,bq->bp", shell_inverse.reshape(NSB, BLK, BLK), struct_total, precision=highest).reshape(-1)
    return fluid_state, struct_state
```

```python
import functools

import jax
import jax.numpy as jnp
from jax import lax
from jax.experimental import pallas as pl
from jax.experimental.pallas import tpu as pltpu
from jax.sharding import PartitionSpec as P

NVAR = 5
FACES = 6
TMAP = 3
DOF = 6
BLK = 96
NB = 4
SWEEPS = 6
ITERS = 2
CELL = 512
HALF = 256
SURF = 256
LANES = 128
FLUID = 16
STRUCT = 8
DEVS = FLUID * STRUCT
PIECE_NODES = 32
PIECE = PIECE_NODES * 3
ROW = 3 * LANES
BOTH = ("fluid", "struct")

G_FACE = 0
G_DIAG = 30
G_RHS = 35
G_STATE = 36
G_LOAD = 38
G_MISC = 41
G_ALL = 44
M_INDEX = 0
M_NODE = 6
M_WEIGHT = 9
M_CELL = 12
M_LIVE = 13

f32 = jnp.float32
bf16 = jnp.bfloat16
NN = (((1,), (0,)), ((), ()))
NT = (((1,), (1,)), ((), ()))


def split(x):
    hi = x.astype(bf16)
    return hi, (x - hi.astype(f32)).astype(bf16)


def split3(x):
    hi = x.astype(bf16)
    rest = x - hi.astype(f32)
    mid = rest.astype(bf16)
    return hi, mid, (rest - mid.astype(f32)).astype(bf16)


def dot(a, b, dims):
    return lax.dot_general(a, b, dims, preferred_element_type=f32)


def iota(shape, axis):
    return lax.broadcasted_iota(jnp.int32, shape, axis)


def one_hot(mask):
    return jnp.where(mask, f32(1.0), f32(0.0)).astype(bf16)


def component_perm(half):
    row, col = iota((PIECE, BLK), 0), iota((PIECE, BLK), 1)
    dof = col % DOF
    return one_hot((dof < 3) & (row == dof * PIECE_NODES + half * 16 + col // DOF))


def live_row(count):
    return jnp.where(iota((1, SURF), 1) < count, f32(1.0), f32(0.0))


def by_device(node):
    return ((node >> 5) & 15) * STRUCT + (node >> 9)


def by_piece(node):
    return node >> 5


def pack_kernel(face, diag, rhs, state, load, index, node, weight, cell, count, adjoint,
                pack_low, pack_high, diag_t, rows):
    for v in range(NVAR):
        for u in range(NVAR):
            diag_t[u, v:v + 1, :] = diag[v, u:u + 1, :]
    live = live_row(count[0])
    for pack, lo in ((pack_low, HALF), (pack_high, 0)):
        cols = slice(lo, lo + HALF)
        pack[G_FACE:G_DIAG] = face[:, :, cols]
        pack[G_DIAG:G_RHS] = diag_t[:, :, cols]
        pack[G_RHS] = rhs[:, cols]
        pack[G_STATE] = state[:, 0:HALF]
        pack[G_STATE + 1] = state[:, HALF:CELL]
        pack[G_LOAD:G_MISC] = load[...]

        def misc(at, value):
            pack[G_MISC + at // 5, at % 5:at % 5 + 1, :] = value

        for k in range(FACES):
            misc(M_INDEX + k, index[k:k + 1, cols].astype(f32))
        for t in range(TMAP):
            misc(M_NODE + t, node[t:t + 1, :].astype(f32))
            misc(M_WEIGHT + t, weight[t:t + 1, :])
        misc(M_CELL, cell[...].astype(f32))
        misc(M_LIVE, live)
        misc(14, jnp.zeros((1, SURF), f32))
    first, second = adjoint[:, 0:BLK], adjoint[:, BLK:2 * BLK]
    comps = jnp.zeros((FLUID, PIECE), f32)
    for half, part in enumerate((first, second)):
        perm = component_perm(half)
        for term in split3(part):
            comps += dot(term, perm, NT)
    for s in range(STRUCT):
        rows[s, :, 0:BLK] = first
        rows[s, :, LANES:LANES + BLK] = second
        rows[s, :, 2 * LANES:2 * LANES + PIECE] = comps
        for j in range(3):
            rows[s, :, j * LANES + BLK:(j + 1) * LANES] = jnp.zeros((FLUID, LANES - BLK), f32)


def couple(struct_t, node, weight, load, cell, live, row_of, cells, base):
    parts = []
    for t in range(TMAP):
        pick = one_hot(iota((DEVS, SURF), 0) == row_of(node[t]))
        found = dot(struct_t[0], pick, NN) + dot(struct_t[1], pick, NN)
        gain = jnp.where(iota((PIECE_NODES, SURF), 0) == (node[t] & 31), weight[t], f32(0.0))
        parts.append((found, gain))
    shown = None
    for j in range(3):
        total = None
        for found, gain in parts:
            term = found[j * PIECE_NODES:(j + 1) * PIECE_NODES] * gain
            total = term if total is None else total + term
        moved = jnp.sum(total, axis=0, keepdims=True)
        term = load[j] * moved
        shown = term if shown is None else shown + term
    shown = shown * live
    at = one_hot(iota((cells, SURF), 0) + base == cell)
    hi, lo = split(shown)
    return dot(hi, at, NT) + dot(lo, at, NT)


def fluid_kernel(first, whole_rows, last, from_pack, *refs):
    refs = list(refs)
    take = lambda n: [refs.pop(0) for _ in range(n)]
    face, diag_t, rhs, index, low, high, state = take(7)
    if not from_pack:
        state_low, state_high = take(2)
    if first:
        struct_rows, load = take(2)
    else:
        (coupled,) = take(1)
    if first or last:
        node, weight, cell, count = take(4)
    if last:
        (disp,) = take(1)
    (out,) = take(1)
    if first:
        (coupled,) = take(1)
    if last:
        (shares,) = take(1)
    x0, x1, picks = take(3)

    x0[0:NVAR, CELL:2 * CELL] = state[...]
    if from_pack:
        for pack, at in ((low, 0), (high, 2 * CELL)):
            x0[0:NVAR, at:at + HALF] = pack[G_STATE]
            x0[0:NVAR, at + HALF:at + CELL] = pack[G_STATE + 1]
    else:
        x0[0:NVAR, 0:CELL] = state_low[...]
        x0[0:NVAR, 2 * CELL:3 * CELL] = state_high[...]

    def misc(pack, at):
        return pack[G_MISC + at // 5, at % 5:at % 5 + 1, :]

    picks[FACES:8, :] = jnp.zeros((8 - FACES, 2 * CELL), jnp.int32)
    picks[0:FACES, HALF:HALF + CELL] = index[...]
    for k in range(FACES):
        picks[k:k + 1, 0:HALF] = misc(low, M_INDEX + k).astype(jnp.int32) - CELL
        picks[k:k + 1, HALF + CELL:2 * CELL] = misc(high, M_INDEX + k).astype(jnp.int32) + CELL

    if first:
        turned = jnp.transpose(struct_rows[:, 2 * LANES:3 * LANES])
        struct_t = split(turned)
        row_of = by_piece if whole_rows else by_device
        coupled[:, HALF:HALF + CELL] = couple(
            struct_t,
            [node[t:t + 1, :] for t in range(TMAP)],
            [weight[t:t + 1, :] for t in range(TMAP)],
            [load[j] for j in range(3)],
            cell[...], live_row(count[0]), row_of, CELL, 0,
        )
        for pack, at, base in ((low, 0, HALF), (high, HALF + CELL, 0)):
            coupled[:, at:at + HALF] = couple(
                struct_t,
                [misc(pack, M_NODE + t).astype(jnp.int32) for t in range(TMAP)],
                [misc(pack, M_WEIGHT + t) for t in range(TMAP)],
                [pack[G_LOAD + j] for j in range(3)],
                misc(pack, M_CELL).astype(jnp.int32), misc(pack, M_LIVE), row_of, HALF, base,
            )

    def sweep(source, shift, at):
        if at < 0:
            lane = at + HALF
            block = lambda i: low[G_FACE + i, :, lane:lane + LANES]
            inv = lambda u: low[G_DIAG + u, :, lane:lane + LANES]
            right = low[G_RHS, :, lane:lane + LANES]
        elif at >= CELL:
            lane = at - CELL
            block = lambda i: high[G_FACE + i, :, lane:lane + LANES]
            inv = lambda u: high[G_DIAG + u, :, lane:lane + LANES]
            right = high[G_RHS, :, lane:lane + LANES]
        else:
            block = lambda i: face[i, :, at:at + LANES]
            inv = lambda u: diag_t[u, :, at:at + LANES]
            right = rhs[:, at:at + LANES]
        place = picks[:, at + HALF:at + HALF + LANES] - at
        lane_of, chunk_of = place & (LANES - 1), place >> 7
        terms = None
        for u in range(NVAR):
            near = None
            for o in range(5):
                begin = at - HALF + o * LANES + shift
                row = jnp.broadcast_to(source[u:u + 1, begin:begin + LANES], (8, LANES))
                found = jnp.take_along_axis(row, lane_of, axis=1, mode="promise_in_bounds")
                near = found if near is None else jnp.where(chunk_of == o, found, near)
            for k in range(FACES):
                term = block(k * NVAR + u) * near[k:k + 1, :]
                terms = term if terms is None else terms + term
        left = right + coupled[:, at + HALF:at + HALF + LANES] - terms
        new = None
        for u in range(NVAR):
            term = inv(u) * left[u:u + 1, :]
            new = term if new is None else new + term
        return new

    for at in range(-HALF, CELL + HALF, LANES):
        x1[0:NVAR, at + HALF:at + HALF + LANES] = sweep(x0, CELL, at)
    for at in range(0, CELL, LANES):
        out[:, at:at + LANES] = sweep(x1, HALF, at)

    if last:
        at = one_hot(iota((CELL, SURF), 0) == cell[...])
        hi, lo = split(out[...])
        surface = dot(hi, at, NN) + dot(lo, at, NN)
        sens = None
        for v in range(NVAR):
            term = disp[v] * surface[v:v + 1, :]
            sens = term if sens is None else sens + term
        sens = sens * live_row(count[0])
        total = None
        for t in range(TMAP):
            nodes = node[t:t + 1, :]
            pick = one_hot(iota((DEVS, SURF), 0) == by_device(nodes))
            gain = jnp.where(iota((PIECE_NODES, SURF), 0) == (nodes & 31),
                             weight[t:t + 1, :], f32(0.0))
            value = jnp.concatenate([gain * sens[j:j + 1, :] for j in range(3)], axis=0)
            for part in split(value):
                term = dot(pick, part, NT)
                total = term if total is None else total + term
        shares[:, 0:PIECE] = total
        shares[:, PIECE:LANES] = jnp.zeros((DEVS, LANES - PIECE), f32)


def shell_kernel(whole_rows, struct_rows, blocks, columns, out):
    for half in range(2):
        total = jnp.zeros((1, BLK), f32)
        for m in range(NB):
            column = columns[m, half]
            piece = column // 2
            row = piece if whole_rows else (piece % FLUID) * STRUCT + piece // FLUID
            line = struct_rows[pl.ds(row, 1), :]
            x = jnp.where(column % 2 == 0, line[:, 0:BLK], line[:, LANES:LANES + BLK])
            x_hi, x_lo = split(x)
            b_hi, b_lo = split(blocks[m, half])
            total += dot(x_hi, b_hi, NN) + dot(x_lo, b_hi, NN) + dot(x_hi, b_lo, NN)
        out[half:half + 1, :] = total


def solve_kernel(received, rhs, shell, inverse, out):
    force = jnp.sum(received[...], axis=0, keepdims=True)[:, 0:PIECE]
    parts = split3(force)
    comps = jnp.zeros((1, PIECE), f32)
    new = []
    for half in range(2):
        perm = component_perm(half)
        load = dot(parts[0], perm, NN) + dot(parts[1], perm, NN) + dot(parts[2], perm, NN)
        right = rhs[half:half + 1, :] + load - shell[half:half + 1, :]
        r_hi, r_lo = split(right)
        i_hi, i_lo = split(inverse[half])
        x = dot(r_hi, i_hi, NT) + dot(r_lo, i_hi, NT) + dot(r_hi, i_lo, NT)
        new.append(x)
        for term in split3(x):
            comps += dot(term, perm, NT)
    count = out.shape[0]
    for j, part in enumerate((new[0], new[1], comps)):
        if (j + 1) * LANES <= out.shape[1]:
            out[:, j * LANES:j * LANES + BLK] = jnp.broadcast_to(part, (count, BLK))
            out[:, j * LANES + BLK:(j + 1) * LANES] = jnp.zeros((count, LANES - BLK), f32)


VMEM = pl.BlockSpec(memory_space=pltpu.VMEM)
SMEM = pl.BlockSpec(memory_space=pltpu.SMEM)


def call(kernel, name, out_shapes, specs, scratch=()):
    return pl.pallas_call(
        kernel,
        name=name,
        out_shape=[jax.ShapeDtypeStruct(s, f32) for s in out_shapes],
        in_specs=specs,
        out_specs=[VMEM] * len(out_shapes),
        scratch_shapes=list(scratch),
        compiler_params=pltpu.CompilerParams(vmem_limit_bytes=48 * 1024 * 1024),
    )


FLUID_SCRATCH = (
    pltpu.VMEM((8, 3 * CELL), f32),
    pltpu.VMEM((8, 2 * CELL), f32),
    pltpu.VMEM((8, 2 * CELL), jnp.int32),
)


def body(
    fluid_adjoint,
    fluid_rhs,
    diag_inverse,
    face_blocks,
    face_index,
    surface_cell,
    surface_count,
    transfer_node,
    transfer_weight,
    load_sens,
    disp_sens,
    struct_adjoint,
    struct_rhs,
    shell_blocks,
    shell_inverse,
    shell_columns,
):
    face = face_blocks.reshape(FACES * NVAR, NVAR, CELL)
    cell = surface_cell.reshape(1, SURF)
    up = [(i, i + 1) for i in range(DEVS - 1)]
    down = [(i + 1, i) for i in range(DEVS - 1)]

    pack_low, pack_high, diag_t, rows = call(
        pack_kernel, "pack",
        [(G_ALL, NVAR, HALF), (G_ALL, NVAR, HALF), (NVAR, NVAR, CELL), (STRUCT, FLUID, ROW)],
        [VMEM] * 9 + [SMEM, VMEM],
    )(face, diag_inverse, fluid_rhs, fluid_adjoint, load_sens, face_index, transfer_node,
      transfer_weight, cell, surface_count, struct_adjoint.reshape(FLUID, 2 * BLK))
    low = lax.ppermute(pack_low, BOTH, up)
    high = lax.ppermute(pack_high, BOTH, down)
    struct_rows = lax.all_to_all(rows, "struct", 0, 0, tiled=True).reshape(DEVS, ROW)

    mine = 2 * lax.axis_index("fluid")
    own = lambda a, axis: lax.dynamic_slice_in_dim(a, mine, 2, axis)
    blocks = own(shell_blocks, 1).reshape(NB, 2, BLK, BLK)
    inverse = own(shell_inverse, 0).reshape(2, BLK, BLK)
    columns = own(shell_columns, 1)
    rhs_rows = own(struct_rhs.reshape(2 * FLUID, BLK), 0)

    state = fluid_adjoint
    for iteration in range(ITERS):
        start = iteration == 0
        (shell,) = call(
            functools.partial(shell_kernel, start), "shell", [(2, BLK)], [VMEM, VMEM, SMEM]
        )(struct_rows, blocks, columns)
        for phase in range(3):
            first, last = phase == 0, phase == 2
            from_pack = start and first
            args = [face, diag_t, fluid_rhs, face_index, low, high, state]
            if not from_pack:
                args += [lax.ppermute(state, BOTH, up), lax.ppermute(state, BOTH, down)]
            args += [struct_rows, load_sens] if first else [coupled]
            specs = [VMEM] * len(args)
            if first or last:
                args += [transfer_node, transfer_weight, cell, surface_count]
                specs += [VMEM] * 3 + [SMEM]
            if last:
                args += [disp_sens]
                specs += [VMEM]
            outs = [(NVAR, CELL)]
            if first:
                outs.append((NVAR, 2 * CELL))
            if last:
                outs.append((DEVS, LANES))
            result = call(
                functools.partial(fluid_kernel, first, start, last, from_pack),
                "fluid", outs, specs, FLUID_SCRATCH,
            )(*args)
            state = result[0]
            if first:
                coupled = result[1]
            if last:
                shares = result[1]
        received = lax.all_to_all(shares, BOTH, 0, 0, tiled=True)
        final = iteration == ITERS - 1
        (solved,) = call(
            solve_kernel, "solve", [(FLUID, 2 * LANES) if final else (DEVS, ROW)], [VMEM] * 4
        )(received, rhs_rows, shell, inverse)
        if final:
            group = lax.all_to_all(solved, "fluid", 0, 0, tiled=True)
            struct_state = group.reshape(FLUID, 2, LANES)[:, :, 0:BLK].reshape(-1)
        else:
            struct_rows = lax.all_to_all(solved, BOTH, 0, 0, tiled=True)
    return (state, struct_state)


def solution(mesh):
    placed = (
        P(None, ("fluid", "struct")),
        P(None, ("fluid", "struct")),
        P(None, None, ("fluid", "struct")),
        P(None, None, None, ("fluid", "struct")),
        P(None, ("fluid", "struct")),
        P(("fluid", "struct")),
        P(("fluid", "struct")),
        P(None, ("fluid", "struct")),
        P(None, ("fluid", "struct")),
        P(None, None, ("fluid", "struct")),
        P(None, None, ("fluid", "struct")),
        P("struct"),
        P("struct"),
        P(None, "struct", None),
        P("struct", None),
        P(None, "struct"),
    )
    return jax.shard_map(
        body,
        mesh=mesh,
        in_specs=placed,
        out_specs=(P(None, ("fluid", "struct")), P("struct")),
        check_vma=False,
    )
```

```python
import functools

import jax
import jax.numpy as jnp
from jax import lax
from jax.experimental import pallas as pl
from jax.experimental.pallas import tpu as pltpu
from jax.sharding import PartitionSpec as P

NVAR = 5
FACES = 6
TMAP = 3
DOF = 6
BLK = 96
NB = 4
CELL = 512
HALF = 256
SURF = 256
LANES = 128
FLUID = 16
STRUCT = 8
DEVS = FLUID * STRUCT
PIECE_NODES = 32
PIECE = PIECE_NODES * 3
BOTH = ("fluid", "struct")
OFFSETS = (-3, -2, -1, 1, 2, 3)
CHUNKS = NVAR * CELL // LANES
SIDE = 5
G_FACE = 0
G_DIAG = 25
G_ALL = 30
R_PLACE = 0
R_RHS = 6
R_STATE = 11
R_OTHER = 16
R_NODE = 21
R_WEIGHT = 24
R_CELL = 27
R_LIVE = 28
R_ALL = 2 * 25

f32 = jnp.float32
bf16 = jnp.bfloat16
NN = (((1,), (0,)), ((), ()))
NT = (((1,), (1,)), ((), ()))


def split(x):
    hi = x.astype(bf16)
    return hi, (x - hi.astype(f32)).astype(bf16)


def split3(x):
    hi = x.astype(bf16)
    rest = x - hi.astype(f32)
    mid = rest.astype(bf16)
    return hi, mid, (rest - mid.astype(f32)).astype(bf16)


def dot(a, b, dims):
    return lax.dot_general(a, b, dims, preferred_element_type=f32)


def iota(shape, axis):
    return lax.broadcasted_iota(jnp.int32, shape, axis)


def one_hot(mask):
    return jnp.where(mask, f32(1.0), f32(0.0)).astype(bf16)


def component_perm(half):
    row, col = iota((PIECE, BLK), 0), iota((PIECE, BLK), 1)
    dof = col % DOF
    return one_hot((dof < 3) & (row == dof * PIECE_NODES + half * 16 + col // DOF))


def live_row(count):
    return jnp.where(iota((1, SURF), 1) < count, f32(1.0), f32(0.0))


def get_row(pack, at, lanes=slice(None)):
    return pack[at // 2, FACES + at % 2:FACES + at % 2 + 1, lanes]


def get_rows(pack, at, count, lanes=slice(None)):
    return jnp.concatenate([get_row(pack, at + i, lanes) for i in range(count)], axis=0)


def spread(part):
    return jnp.concatenate([part, jnp.zeros((part.shape[0], LANES - part.shape[1]), f32)], axis=1)


def components(parts):
    total = None
    for half, part in enumerate(parts):
        perm = component_perm(half)
        for term in split3(part):
            product = dot(term, perm, NT)
            total = product if total is None else total + product
    return total


def by_device(node):
    return ((node >> 5) & 15) * STRUCT + (node >> 9)


def by_piece(node):
    return node >> 5


def start_copies(pairs, sems):
    copies = [pltpu.make_async_copy(s, d, sems.at[i]) for i, (s, d) in enumerate(pairs)]
    for copy in copies:
        copy.start()
    return copies


def pack_kernel(face, diag, rhs, state, load, place, node, weight, cell, adjoint, count,
                own, rows,
                face_v, diag_v, rhs_v, state_v, load_v, place_v, node_v, weight_v, cell_v,
                adjoint_v, own_v, rows_v, sems, out_sems):
    copies = start_copies(
        [(face, face_v), (diag, diag_v), (rhs, rhs_v), (state, state_v), (load, load_v),
         (place, place_v), (node, node_v), (weight, weight_v), (cell, cell_v),
         (adjoint, adjoint_v)], sems)
    for copy in copies:
        copy.wait()
    live = live_row(count[0])
    sent = []
    for half in range(2):
        cols = slice(half * HALF, (half + 1) * HALF)
        other = slice((1 - half) * HALF, (2 - half) * HALF)
        pack = own_v.at[half]

        def put(at, value):
            pack[at // 2, FACES + at % 2:FACES + at % 2 + 1, :] = value

        for u in range(NVAR):
            for v in range(NVAR):
                pack[G_FACE + u * NVAR + v, 0:FACES, :] = face_v[u, v, :, cols]
                pack[G_DIAG + u, v:v + 1, :] = diag_v[v, u:u + 1, cols]
            pack[G_DIAG + u, 5:8, :] = load_v[u]
        shift = iota((1, HALF), 1) // LANES * LANES + half * HALF
        for k in range(FACES):
            put(R_PLACE + k, (place_v[k:k + 1, cols] - shift).astype(f32))
        for v in range(NVAR):
            put(R_RHS + v, rhs_v[v:v + 1, cols])
            put(R_STATE + v, state_v[v:v + 1, cols])
            put(R_OTHER + v, state_v[v:v + 1, other])
        for t in range(TMAP):
            put(R_NODE + t, node_v[t:t + 1, :].astype(f32))
            put(R_WEIGHT + t, weight_v[t:t + 1, :])
        put(R_CELL, cell_v[...].astype(f32))
        put(R_LIVE, live)
        for at in range(R_LIVE + 1, R_ALL):
            put(at, jnp.zeros((1, HALF), f32))
        sent.append(pltpu.make_async_copy(own_v.at[half], own.at[half], out_sems.at[half]))
        sent[-1].start()
    wide = spread(adjoint_v[...])
    for s in range(STRUCT):
        rows_v[s] = wide
    sent.append(pltpu.make_async_copy(rows_v, rows, out_sems.at[2]))
    sent[-1].start()
    for copy in sent:
        copy.wait()


def slots(pack):
    node = get_rows(pack, R_NODE, TMAP).astype(jnp.int32)
    weight = get_rows(pack, R_WEIGHT, TMAP)
    cell = get_row(pack, R_CELL).astype(jnp.int32)
    live = get_row(pack, R_LIVE)
    return node, weight, cell, live


def surface_loads(struct_t, pack, row_of):
    node, weight, cell, live = slots(pack)
    total = [None] * 3
    for t in range(TMAP):
        nodes = node[t:t + 1, :]
        pick = one_hot(iota((DEVS, SURF), 0) == row_of(nodes))
        found = dot(struct_t[0], pick, NN) + dot(struct_t[1], pick, NN)
        gain = jnp.where(iota((PIECE_NODES, SURF), 0) == (nodes & 31), weight[t:t + 1, :], f32(0.0))
        for j in range(3):
            term = found[j * PIECE_NODES:(j + 1) * PIECE_NODES] * gain
            total[j] = term if total[j] is None else total[j] + term
    moved = [jnp.sum(x, axis=0, keepdims=True) * live for x in total]
    shown = []
    for v in range(NVAR):
        term = None
        for j in range(3):
            part = pack[G_DIAG + v, 5 + j:6 + j, :] * moved[j]
            term = part if term is None else term + part
        shown.append(term)
    shown.append(jnp.zeros((8 - NVAR, SURF), f32))
    return split(jnp.concatenate(shown, axis=0))


def fluid_kernel(start, *refs):
    refs = list(refs)
    take = lambda n: [refs.pop(0) for _ in range(n)]
    pack_refs = take(len(PACKS))
    struct_ref, disp_ref = take(2)
    if not start:
        (state_ref,) = take(1)
    out, shares = take(2)
    packs, x0, x1, source, places, struct_v, disp_v, chunks = take(8)
    if not start:
        (state_v,) = take(1)
    (sems,) = take(1)

    side = SIDE
    pairs = [(struct_ref, struct_v)]
    for ref, (at, count) in zip(pack_refs, PACKS):
        pairs.append((ref, packs.at[pl.ds(side + at, count)] if count > 1 else packs.at[side + at]))
    pairs.append((disp_ref, disp_v))
    if not start:
        pairs.append((state_ref, state_v))
    copies = start_copies(pairs, sems)
    for copy in copies:
        copy.wait()

    base = 2 * (side + 1)
    if start:
        for h in range(-side, side + 2):
            wanted = [(h, R_STATE)]
            wanted += [(h - 1, R_OTHER)] * (h == -side) + [(h + 1, R_OTHER)] * (h == side + 1)
            for at, row in wanted:
                for v in range(NVAR):
                    line = get_row(packs.at[side + h], row + v)
                    for c in range(2):
                        x0[base + 2 * at + c, v:v + 1, :] = line[:, c * LANES:(c + 1) * LANES]
    else:
        chunks[...] = struct_v[pl.ds(3, DEVS, stride=4), :]
        for c in range(4):
            x0[base + c, 0:NVAR, :] = state_v[:, c * LANES:(c + 1) * LANES]
            for k, offset in enumerate(OFFSETS):
                row = k * CHUNKS + c * NVAR
                x0[base + 4 * offset + c, 0:NVAR, :] = chunks[row:row + NVAR, :]

    if start:
        parts = [struct_v[pl.ds(half, DEVS, stride=2), :][:, 0:BLK] for half in range(2)]
        struct_t = split(jnp.transpose(spread(components(parts))))
    else:
        struct_t = split(jnp.transpose(struct_v[pl.ds(2, DEVS, stride=4), :]))
    row_of = by_piece if start else by_device
    halves = list(range(-side, side + 2))
    for block in sorted(set(h // 2 for h in halves)):
        present = [h for h in halves if h // 2 == block]
        pack = packs.at[side + present[0]]
        loads = surface_loads(struct_t, pack, row_of)
        cell = get_row(pack, R_CELL).astype(jnp.int32)
        for h in present:
            at = one_hot(iota((HALF, SURF), 0) + (h % 2) * HALF == cell)
            coupled = dot(loads[0], at, NT) + dot(loads[1], at, NT)
            value = coupled[0:NVAR] + get_rows(packs.at[side + h], R_RHS, NVAR)
            place = get_rows(packs.at[side + h], R_PLACE, FACES).astype(jnp.int32)
            for c in range(2):
                lanes = slice(c * LANES, (c + 1) * LANES)
                chunk = 2 * (side + h) + c
                source[chunk, 0:NVAR, :] = value[:, lanes]
                places[chunk, 0:FACES, :] = place[:, lanes]
                places[chunk, FACES:8, :] = jnp.full((8 - FACES, LANES), -1, jnp.int32)

    def sweep_half(x_in, x_out, half, write):
        for c in range(2):
            lanes = slice(c * LANES, (c + 1) * LANES)
            chunk = 2 * half + c
            place = places[chunk]
            lane_of, chunk_of = place & (LANES - 1), place >> 7
            masks = [chunk_of == o for o in range(5)]
            sums = [None] * NVAR
            for u in range(NVAR):
                near = None
                for o in range(5):
                    row = jnp.broadcast_to(x_in[chunk + o, u:u + 1, :], (8, LANES))
                    found = jnp.take_along_axis(row, lane_of, axis=1, mode="promise_in_bounds")
                    near = jnp.where(masks[o], found, f32(0.0) if o == 0 else near)
                for v in range(NVAR):
                    term = packs[half, G_FACE + u * NVAR + v, :, lanes] * near
                    sums[v] = term if sums[v] is None else sums[v] + term
            new = None
            for u in range(NVAR):
                left = source[chunk, u:u + 1, :] - jnp.sum(sums[u], axis=0, keepdims=True)
                term = packs[half, G_DIAG + u, 0:NVAR, lanes] * left
                new = term if new is None else new + term
            write(chunk, new)

    x_in, x_out = x0, x1
    for step in range(SIDE + 1):
        reach = SIDE - step
        done = step == SIDE
        if done:
            def write(chunk, new):
                at = (chunk - 2 * side) * LANES
                out[:, at:at + LANES] = new
        else:
            def write(chunk, new, x_out=x_out):
                x_out[chunk + 2, 0:NVAR, :] = new
        first, end = side - reach, side + 2 + reach
        for half in range(first, end):
            sweep_half(x_in, x_out, half, write)
        x_in, x_out = x_out, x_in

    node, weight, cell, live = slots(packs.at[side])
    at = one_hot(iota((CELL, SURF), 0) == cell)
    hi, lo = split(out[...])
    surface = dot(hi, at, NN) + dot(lo, at, NN)
    sens = None
    for v in range(NVAR):
        term = disp_v[v] * surface[v:v + 1, :]
        sens = term if sens is None else sens + term
    sens = sens * live
    total = None
    for t in range(TMAP):
        nodes = node[t:t + 1, :]
        pick = one_hot(iota((DEVS, SURF), 0) == by_device(nodes))
        gain = jnp.where(iota((PIECE_NODES, SURF), 0) == (nodes & 31),
                         weight[t:t + 1, :], f32(0.0))
        value = jnp.concatenate([gain * sens[j:j + 1, :] for j in range(3)], axis=0)
        for part in split(value):
            term = dot(pick, part, NT)
            total = term if total is None else total + term
    wide = spread(total)
    if not start:
        shares[...] = wide
    else:
        shares[pl.ds(0, DEVS, stride=2), :] = wide
        for k in range(len(OFFSETS)):
            for c in range(4):
                row = k * CHUNKS + c * NVAR
                chunks[row:row + NVAR, :] = out[:, c * LANES:(c + 1) * LANES]
        rest = len(OFFSETS) * CHUNKS
        chunks[rest:DEVS, :] = jnp.zeros((DEVS - rest, LANES), f32)
        shares[pl.ds(1, DEVS, stride=2), :] = chunks[...]


PACKS = ((0, 2), (-2, 2), (2, 2), (-4, 2), (4, 2), (-5, 1), (6, 1))


def fluid(start, packs, struct_rows, disp, state=None):
    args = list(packs) + [struct_rows, disp] + ([] if start else [state])
    halves = 2 * SIDE + 2
    scratch = [
        pltpu.VMEM((halves, G_ALL, 8, HALF), f32),
        pltpu.VMEM((2 * halves + 4, 8, LANES), f32),
        pltpu.VMEM((2 * halves + 4, 8, LANES), f32),
        pltpu.VMEM((2 * halves, 8, LANES), f32),
        pltpu.VMEM((2 * halves, 8, LANES), jnp.int32),
        pltpu.VMEM(struct_rows.shape, f32),
        pltpu.VMEM((NVAR, 3, SURF), f32),
        pltpu.VMEM((DEVS, LANES), f32),
    ]
    if not start:
        scratch.append(pltpu.VMEM((NVAR, CELL), f32))
    scratch.append(pltpu.SemaphoreType.DMA((len(args),)))
    outs = [(NVAR, CELL), (2 * DEVS if start else DEVS, LANES)]
    return call(functools.partial(fluid_kernel, start), "fluid", outs, [ANY] * len(args), scratch, vmem=63)(*args)


def shell_kernel(whole_rows, struct_rows, blocks, columns, out):
    for half in range(2):
        total = jnp.zeros((1, BLK), f32)
        for m in range(NB):
            column = columns[m, half]
            piece = column // 2
            row = (piece % FLUID) * STRUCT + piece // FLUID
            line = column if whole_rows else 4 * row + column % 2
            x = struct_rows[pl.ds(line, 1), :][:, 0:BLK]
            x_hi, x_lo = split(x)
            b_hi, b_lo = split(blocks[m, half])
            total += dot(x_hi, b_hi, NN) + dot(x_lo, b_hi, NN) + dot(x_hi, b_lo, NN)
        out[half:half + 1, :] = total


def solve_kernel(received, rhs, shell, inverse, relay, out, *padded):
    start = bool(padded)
    lines = received[pl.ds(0, DEVS, stride=2), :] if start else received[...]
    parts = split3(jnp.sum(lines, axis=0, keepdims=True)[:, 0:PIECE])
    new = []
    for half in range(2):
        perm = component_perm(half)
        load = dot(parts[0], perm, NN) + dot(parts[1], perm, NN) + dot(parts[2], perm, NN)
        right = rhs[half:half + 1, :] + load - shell[half:half + 1, :]
        r_hi, r_lo = split(right)
        i_hi, i_lo = split(inverse[half])
        new.append(dot(r_hi, i_hi, NT) + dot(r_lo, i_hi, NT) + dot(r_hi, i_lo, NT))
    rows = new + [components(new)] if start else new
    every = 4 if start else 2
    count = out.shape[0] // every
    for j, part in enumerate(rows):
        out[pl.ds(j, count, stride=every), :] = jnp.broadcast_to(spread(part), (count, LANES))
    if start:
        (lined,) = padded
        lined[0:8, :] = jnp.zeros((8, LANES), f32)
        lined[8:8 + DEVS, :] = received[pl.ds(1, DEVS, stride=2), :]
        lined[8 + DEVS:16 + DEVS, :] = jnp.zeros((8, LANES), f32)
        for k, offset in enumerate(OFFSETS):
            @pl.when(relay[0] == k)
            def _():
                out[pl.ds(3, DEVS, stride=4), :] = lined[8 + offset:8 + offset + DEVS, :]

        @pl.when(relay[0] >= len(OFFSETS))
        def _():
            out[pl.ds(3, DEVS, stride=4), :] = jnp.zeros((DEVS, LANES), f32)


VMEM = pl.BlockSpec(memory_space=pltpu.VMEM)
SMEM = pl.BlockSpec(memory_space=pltpu.SMEM)
ANY = pl.BlockSpec(memory_space=pltpu.HBM)


def call(kernel, name, out_shapes, specs, scratch=(), out_specs=None, vmem=16):
    return pl.pallas_call(
        kernel,
        name=name,
        out_shape=[jax.ShapeDtypeStruct(s, f32) for s in out_shapes],
        in_specs=specs,
        out_specs=out_specs or [VMEM] * len(out_shapes),
        scratch_shapes=list(scratch),
        compiler_params=pltpu.CompilerParams(vmem_limit_bytes=vmem * 1024 * 1024),
    )


def body(
    fluid_adjoint,
    fluid_rhs,
    diag_inverse,
    face_blocks,
    face_index,
    surface_cell,
    surface_count,
    transfer_node,
    transfer_weight,
    load_sens,
    disp_sens,
    struct_adjoint,
    struct_rhs,
    shell_blocks,
    shell_inverse,
    shell_columns,
):
    def shift(value, by):
        pairs = [(i, i + by) for i in range(DEVS) if 0 <= i + by < DEVS]
        return lax.ppermute(value, BOTH, pairs)

    sizes = [(NVAR, NVAR, FACES, CELL), (NVAR, NVAR, CELL), (NVAR, CELL), (NVAR, CELL),
             (NVAR, 3, SURF), (FACES, CELL), (TMAP, SURF), (TMAP, SURF), (1, SURF),
             (2 * FLUID, BLK)]
    kinds = [f32] * 5 + [jnp.int32] * 2 + [f32, jnp.int32, f32]
    own_shape = (2, G_ALL, 8, HALF)
    rows_shape = (STRUCT, 2 * FLUID, LANES)
    own, rows = call(
        pack_kernel, "pack", [own_shape, rows_shape], [ANY] * 10 + [SMEM],
        [pltpu.VMEM(s, k) for s, k in zip(sizes, kinds)]
        + [pltpu.VMEM(own_shape, f32), pltpu.VMEM(rows_shape, f32),
           pltpu.SemaphoreType.DMA((10,)), pltpu.SemaphoreType.DMA((3,))],
        [ANY] * 2, vmem=63,
    )(face_blocks.transpose(1, 2, 0, 3), diag_inverse, fluid_rhs, fluid_adjoint,
      load_sens.transpose(1, 0, 2), face_index, transfer_node, transfer_weight,
      surface_cell.reshape(1, SURF), struct_adjoint.reshape(2 * FLUID, BLK), surface_count)
    low = shift(own, 1)
    high = shift(own, -1)
    low_two = shift(own, 2)
    high_two = shift(own, -2)
    struct_rows = lax.all_to_all(rows, "struct", 0, 0, tiled=True).reshape(2 * DEVS, LANES)

    mine = 2 * lax.axis_index("fluid")
    take = lambda a, axis: lax.dynamic_slice_in_dim(a, mine, 2, axis)
    blocks = take(shell_blocks, 1).reshape(NB, 2, BLK, BLK)
    inverse = take(shell_inverse, 0).reshape(2, BLK, BLK)
    columns = take(shell_columns, 1)
    rhs_rows = take(struct_rhs.reshape(2 * FLUID, BLK), 0)

    packs = [own, low, high, low_two, high_two, shift(low[1], 2), shift(high[0], -2)]
    relay = ((lax.axis_index(BOTH)) // CHUNKS).astype(jnp.int32).reshape(1)

    def shell(struct_rows, start):
        (terms,) = call(
            functools.partial(shell_kernel, start), "shell", [(2, BLK)], [VMEM, VMEM, SMEM]
        )(struct_rows, blocks, columns)
        return terms

    def solve(shares, terms, shape, scratch):
        received = lax.all_to_all(shares, BOTH, 0, 0, tiled=True)
        (solved,) = call(solve_kernel, "solve", [shape], [VMEM] * 4 + [SMEM], scratch)(
            received, rhs_rows, terms, inverse, relay)
        return solved

    terms = shell(struct_rows, True)
    state, shares = fluid(True, packs, struct_rows, disp_sens)
    solved = solve(shares, terms, (4 * DEVS, LANES), [pltpu.VMEM((DEVS + 16, LANES), f32)])
    struct_rows = lax.all_to_all(solved, BOTH, 0, 0, tiled=True)
    terms = shell(struct_rows, False)
    state, shares = fluid(False, packs, struct_rows, disp_sens, state)
    solved = solve(shares, terms, (2 * FLUID, LANES), [])
    group = lax.all_to_all(solved, "fluid", 0, 0, tiled=True)
    return (state, group[:, 0:BLK].reshape(-1))


def solution(mesh):
    placed = (
        P(None, ("fluid", "struct")),
        P(None, ("fluid", "struct")),
        P(None, None, ("fluid", "struct")),
        P(None, None, None, ("fluid", "struct")),
        P(None, ("fluid", "struct")),
        P(("fluid", "struct")),
        P(("fluid", "struct")),
        P(None, ("fluid", "struct")),
        P(None, ("fluid", "struct")),
        P(None, None, ("fluid", "struct")),
        P(None, None, ("fluid", "struct")),
        P("struct"),
        P("struct"),
        P(None, "struct", None),
        P("struct", None),
        P(None, "struct"),
    )
    return jax.shard_map(
        body,
        mesh=mesh,
        in_specs=placed,
        out_specs=(P(None, ("fluid", "struct")), P("struct")),
        check_vma=False,
    )
```

```python
import functools

import jax
import jax.numpy as jnp
from jax import lax
from jax.experimental import pallas as pl
from jax.experimental.pallas import tpu as pltpu
from jax.sharding import PartitionSpec as P

NVAR = 5
FACES = 6
TMAP = 3
DOF = 6
BLK = 96
NB = 4
CELL = 512
HALF = 256
SURF = 256
LANES = 128
FLUID = 16
STRUCT = 8
DEVS = FLUID * STRUCT
PIECE_NODES = 32
PIECE = PIECE_NODES * 3
BOTH = ("fluid", "struct")
OFFSETS = (-3, -2, -1, 1, 2, 3)
CHUNKS = NVAR * CELL // LANES
SIDE = 5
G_FACE = 0
G_DIAG = 25
G_ALL = 30
R_PLACE = 0
R_RHS = 6
R_STATE = 11
R_OTHER = 16
R_NODE = 21
R_WEIGHT = 24
R_CELL = 27
R_LIVE = 28
R_DISP = 29
R_ALL = 2 * 25

f32 = jnp.float32
bf16 = jnp.bfloat16
NN = (((1,), (0,)), ((), ()))
NT = (((1,), (1,)), ((), ()))


def split(x):
    hi = x.astype(bf16)
    return hi, (x - hi.astype(f32)).astype(bf16)


def split3(x):
    hi = x.astype(bf16)
    rest = x - hi.astype(f32)
    mid = rest.astype(bf16)
    return hi, mid, (rest - mid.astype(f32)).astype(bf16)


def stack(x):
    return jnp.concatenate([x_half.astype(f32) for x_half in split(x)], axis=0).astype(bf16)


def fold(product):
    rows = product.shape[0] // 2
    return product[0:rows] + product[rows:2 * rows]


def dot(a, b, dims):
    return lax.dot_general(a, b, dims, preferred_element_type=f32)


def iota(shape, axis):
    return lax.broadcasted_iota(jnp.int32, shape, axis)


def one_hot(mask):
    return jnp.where(mask, f32(1.0), f32(0.0)).astype(bf16)


def component_perm(half):
    row, col = iota((PIECE, BLK), 0), iota((PIECE, BLK), 1)
    dof = col % DOF
    return one_hot((dof < 3) & (row == dof * PIECE_NODES + half * 16 + col // DOF))


def live_row(count):
    return jnp.where(iota((1, SURF), 1) < count, f32(1.0), f32(0.0))


def get_row(pack, at, lanes=slice(None)):
    return pack[at // 2, FACES + at % 2:FACES + at % 2 + 1, lanes]


def get_rows(pack, at, count, lanes=slice(None)):
    return jnp.concatenate([get_row(pack, at + i, lanes) for i in range(count)], axis=0)


def spread(part):
    return jnp.concatenate([part, jnp.zeros((part.shape[0], LANES - part.shape[1]), f32)], axis=1)


def components(parts):
    total = None
    for half, part in enumerate(parts):
        perm = component_perm(half)
        for term in split3(part):
            product = dot(term, perm, NT)
            total = product if total is None else total + product
    return total


def by_device(node):
    return ((node >> 5) & 15) * STRUCT + (node >> 9)


def by_piece(node):
    return node >> 5


def start_copies(pairs, sems):
    copies = [pltpu.make_async_copy(s, d, sems.at[i]) for i, (s, d) in enumerate(pairs)]
    for copy in copies:
        copy.start()
    return copies


def pack_kernel(face, diag, rhs, state, load, place, node, weight, cell, disp, count,
                own,
                face_v, diag_v, rhs_v, state_v, load_v, place_v, node_v, weight_v, cell_v,
                disp_v, own_v, sems, out_sems):
    copies = start_copies(
        [(face, face_v), (diag, diag_v), (rhs, rhs_v), (state, state_v), (load, load_v),
         (place, place_v), (node, node_v), (weight, weight_v), (cell, cell_v),
         (disp, disp_v)], sems)
    for copy in copies:
        copy.wait()
    live = live_row(count[0])
    sent = []
    for half in range(2):
        cols = slice(half * HALF, (half + 1) * HALF)
        other = slice((1 - half) * HALF, (2 - half) * HALF)
        pack = own_v.at[half]

        def put(at, value):
            pack[at // 2, FACES + at % 2:FACES + at % 2 + 1, :] = value

        for u in range(NVAR):
            for v in range(NVAR):
                pack[G_FACE + u * NVAR + v, 0:FACES, :] = face_v[u, v, :, cols]
                pack[G_DIAG + u, v:v + 1, :] = diag_v[v, u:u + 1, cols]
            pack[G_DIAG + u, 5:8, :] = load_v[u]
        shift = iota((1, HALF), 1) // LANES * LANES + half * HALF
        for k in range(FACES):
            put(R_PLACE + k, (place_v[k:k + 1, cols] - shift).astype(f32))
        for v in range(NVAR):
            put(R_RHS + v, rhs_v[v:v + 1, cols])
            put(R_STATE + v, state_v[v:v + 1, cols])
            put(R_OTHER + v, state_v[v:v + 1, other])
        for t in range(TMAP):
            put(R_NODE + t, node_v[t:t + 1, :].astype(f32))
            put(R_WEIGHT + t, weight_v[t:t + 1, :])
        put(R_CELL, cell_v[...].astype(f32))
        put(R_LIVE, live)
        for v in range(NVAR):
            for j in range(3):
                put(R_DISP + 3 * v + j, disp_v[v, j:j + 1, :])
        for at in range(R_DISP + 3 * NVAR, R_ALL):
            put(at, jnp.zeros((1, HALF), f32))
        sent.append(pltpu.make_async_copy(own_v.at[half], own.at[half], out_sems.at[half]))
        sent[-1].start()
    for copy in sent:
        copy.wait()


def slots(pack):
    node = get_rows(pack, R_NODE, TMAP).astype(jnp.int32)
    weight = get_rows(pack, R_WEIGHT, TMAP)
    cell = get_row(pack, R_CELL).astype(jnp.int32)
    live = get_row(pack, R_LIVE)
    return node, weight, cell, live


def surface_loads(struct_t, pack, row_of):
    node, weight, cell, live = slots(pack)
    total = [None] * 3
    for t in range(TMAP):
        nodes = node[t:t + 1, :]
        pick = one_hot(iota((DEVS, SURF), 0) == row_of(nodes))
        found = fold(dot(struct_t, pick, NN))
        gain = jnp.where(iota((PIECE_NODES, SURF), 0) == (nodes & 31), weight[t:t + 1, :], f32(0.0))
        for j in range(3):
            term = found[j * PIECE_NODES:(j + 1) * PIECE_NODES] * gain
            total[j] = term if total[j] is None else total[j] + term
    moved = [jnp.sum(x, axis=0, keepdims=True) * live for x in total]
    shown = []
    for v in range(NVAR):
        term = None
        for j in range(3):
            part = pack[G_DIAG + v, 5 + j:6 + j, :] * moved[j]
            term = part if term is None else term + part
        shown.append(term)
    shown.append(jnp.zeros((8 - NVAR, SURF), f32))
    return stack(jnp.concatenate(shown, axis=0))


def fluid_kernel(start, *refs):
    refs = list(refs)
    take = lambda n: [refs.pop(0) for _ in range(n)]
    pack_refs = take(len(PACKS))
    (struct_v,) = take(1)
    if not start:
        (state_v,) = take(1)
    out, shares = take(2)
    x0, x1, source, places, chunks = take(5)

    side = SIDE
    packs = {}
    for ref, (at, count) in zip(pack_refs, PACKS):
        for i in range(count):
            packs[side + at + i] = ref.at[i] if count > 1 else ref

    base = 2 * (side + 1)
    if not start:
        chunks[...] = struct_v[pl.ds(3, DEVS, stride=4), :]
        for c in range(4):
            x0[base + c, 0:NVAR, :] = state_v[:, c * LANES:(c + 1) * LANES]
            for k, offset in enumerate(OFFSETS):
                row = k * CHUNKS + c * NVAR
                x0[base + 4 * offset + c, 0:NVAR, :] = chunks[row:row + NVAR, :]

    if start:
        parts = [struct_v[pl.ds(half, DEVS, stride=2), :][:, 0:BLK] for half in range(2)]
        struct_t = stack(jnp.transpose(spread(components(parts))))
    else:
        struct_t = stack(jnp.transpose(struct_v[pl.ds(2, DEVS, stride=4), :]))
    row_of = by_piece if start else by_device
    for which, (begin, count) in enumerate(PACKS):
        present = list(range(begin, begin + count))
        pack = packs[side + present[0]]
        loads = surface_loads(struct_t, pack, row_of)
        cell = get_row(pack, R_CELL).astype(jnp.int32)
        for h in present:
            at = one_hot(iota((HALF, SURF), 0) + (h % 2) * HALF == cell)
            coupled = fold(dot(loads, at, NT))
            value = coupled[0:NVAR] + get_rows(packs[side + h], R_RHS, NVAR)
            place = get_rows(packs[side + h], R_PLACE, FACES).astype(jnp.int32)
            for c in range(2):
                lanes = slice(c * LANES, (c + 1) * LANES)
                chunk = 2 * (side + h) + c
                source[chunk, 0:NVAR, :] = value[:, lanes]
                places[chunk, 0:FACES, :] = place[:, lanes]
                places[chunk, FACES:8, :] = jnp.full((8 - FACES, LANES), -1, jnp.int32)
            if start:
                wanted = [(h, R_STATE)]
                wanted += [(h - 1, R_OTHER)] * (h == -side)
                wanted += [(h + 1, R_OTHER)] * (h == side + 1)
                for to, row in wanted:
                    lines = get_rows(packs[side + h], row, NVAR)
                    for c in range(2):
                        x0[base + 2 * to + c, 0:NVAR, :] = lines[:, c * LANES:(c + 1) * LANES]

    def sweep_half(x_in, x_out, half, write):
        for c in range(2):
            lanes = slice(c * LANES, (c + 1) * LANES)
            chunk = 2 * half + c
            place = places[chunk]
            lane_of, chunk_of = place & (LANES - 1), place >> 7
            masks = [chunk_of == o for o in range(5)]
            sums = [None] * NVAR
            for u in range(NVAR):
                near = None
                for o in range(5):
                    row = jnp.broadcast_to(x_in[chunk + o, u:u + 1, :], (8, LANES))
                    found = jnp.take_along_axis(row, lane_of, axis=1, mode="promise_in_bounds")
                    near = jnp.where(masks[o], found, f32(0.0) if o == 0 else near)
                for v in range(NVAR):
                    term = packs[half][G_FACE + u * NVAR + v, :, lanes] * near
                    sums[v] = term if sums[v] is None else sums[v] + term
            new = None
            for u in range(NVAR):
                left = source[chunk, u:u + 1, :] - jnp.sum(sums[u], axis=0, keepdims=True)
                term = packs[half][G_DIAG + u, 0:NVAR, lanes] * left
                new = term if new is None else new + term
            write(chunk, new)

    x_in, x_out = x0, x1
    for step in range(SIDE + 1):
        reach = SIDE - step
        done = step == SIDE
        if done:
            def write(chunk, new):
                at = (chunk - 2 * side) * LANES
                out[:, at:at + LANES] = new
        else:
            def write(chunk, new, x_out=x_out):
                x_out[chunk + 2, 0:NVAR, :] = new
        first, end = side - reach, side + 2 + reach
        for half in range(first, end):
            sweep_half(x_in, x_out, half, write)
        x_in, x_out = x_out, x_in

    node, weight, cell, live = slots(packs[side])
    at = one_hot(iota((CELL, SURF), 0) == cell)
    state = jnp.concatenate([out[...], jnp.zeros((8 - NVAR, CELL), f32)], axis=0)
    surface = fold(dot(stack(state), at, NN))
    sens = None
    for v in range(NVAR):
        term = get_rows(packs[side], R_DISP + 3 * v, 3) * surface[v:v + 1, :]
        sens = term if sens is None else sens + term
    sens = sens * live
    total = None
    for t in range(TMAP):
        nodes = node[t:t + 1, :]
        pick = one_hot(iota((DEVS, SURF), 0) == by_device(nodes))
        gain = jnp.where(iota((PIECE_NODES, SURF), 0) == (nodes & 31),
                         weight[t:t + 1, :], f32(0.0))
        value = jnp.concatenate([gain * sens[j:j + 1, :] for j in range(3)], axis=0)
        term = dot(pick, stack(value), NT)
        total = term if total is None else total + term
    wide = spread(total[:, 0:PIECE] + total[:, PIECE:2 * PIECE])
    if not start:
        shares[...] = wide
    else:
        shares[pl.ds(0, DEVS, stride=2), :] = wide
        for k in range(len(OFFSETS)):
            for c in range(4):
                row = k * CHUNKS + c * NVAR
                chunks[row:row + NVAR, :] = out[:, c * LANES:(c + 1) * LANES]
        rest = len(OFFSETS) * CHUNKS
        chunks[rest:DEVS, :] = jnp.zeros((DEVS - rest, LANES), f32)
        shares[pl.ds(1, DEVS, stride=2), :] = chunks[...]


PACKS = ((0, 2), (-2, 2), (2, 2), (-4, 2), (4, 2), (-5, 1), (6, 1))


def fluid(start, packs, struct_rows, state=None):
    args = list(packs) + [struct_rows] + ([] if start else [state])
    halves = 2 * SIDE + 2
    scratch = [
        pltpu.VMEM((2 * halves + 4, 8, LANES), f32),
        pltpu.VMEM((2 * halves + 4, 8, LANES), f32),
        pltpu.VMEM((2 * halves, 8, LANES), f32),
        pltpu.VMEM((2 * halves, 8, LANES), jnp.int32),
        pltpu.VMEM((DEVS, LANES), f32),
    ]
    outs = [(NVAR, CELL), (2 * DEVS if start else DEVS, LANES)]
    return call(functools.partial(fluid_kernel, start), "fluid", outs, [VMEM] * len(args), scratch)(*args)


def shell_kernel(whole_rows, struct_rows, blocks, columns, out):
    for half in range(2):
        total = jnp.zeros((1, BLK), f32)
        for m in range(NB):
            column = columns[m, half]
            piece = column // 2
            row = (piece % FLUID) * STRUCT + piece // FLUID
            line = column if whole_rows else 4 * row + column % 2
            x = struct_rows[pl.ds(line, 1), :][:, 0:BLK]
            x_hi, x_lo = split(x)
            b_hi, b_lo = split(blocks[m, half])
            total += dot(x_hi, b_hi, NN) + dot(x_lo, b_hi, NN) + dot(x_hi, b_lo, NN)
        out[half:half + 1, :] = total


def solve_kernel(received, rhs, shell, inverse, relay, out, *padded):
    start = bool(padded)
    lines = received[pl.ds(0, DEVS, stride=2), :] if start else received[...]
    parts = split3(jnp.sum(lines, axis=0, keepdims=True)[:, 0:PIECE])
    new = []
    for half in range(2):
        perm = component_perm(half)
        load = dot(parts[0], perm, NN) + dot(parts[1], perm, NN) + dot(parts[2], perm, NN)
        right = rhs[half:half + 1, :] + load - shell[half:half + 1, :]
        r_hi, r_lo = split(right)
        i_hi, i_lo = split(inverse[half])
        new.append(dot(r_hi, i_hi, NT) + dot(r_lo, i_hi, NT) + dot(r_hi, i_lo, NT))
    rows = new + [components(new)] if start else new
    every = 4 if start else 2
    count = out.shape[0] // every
    for j, part in enumerate(rows):
        out[pl.ds(j, count, stride=every), :] = jnp.broadcast_to(spread(part), (count, LANES))
    if start:
        (lined,) = padded
        lined[0:8, :] = jnp.zeros((8, LANES), f32)
        lined[8:8 + DEVS, :] = received[pl.ds(1, DEVS, stride=2), :]
        lined[8 + DEVS:16 + DEVS, :] = jnp.zeros((8, LANES), f32)
        for k, offset in enumerate(OFFSETS):
            @pl.when(relay[0] == k)
            def _():
                out[pl.ds(3, DEVS, stride=4), :] = lined[8 + offset:8 + offset + DEVS, :]

        @pl.when(relay[0] >= len(OFFSETS))
        def _():
            out[pl.ds(3, DEVS, stride=4), :] = jnp.zeros((DEVS, LANES), f32)


VMEM = pl.BlockSpec(memory_space=pltpu.VMEM)
SMEM = pl.BlockSpec(memory_space=pltpu.SMEM)
ANY = pl.BlockSpec(memory_space=pltpu.HBM)


def call(kernel, name, out_shapes, specs, scratch=(), out_specs=None, vmem=16):
    return pl.pallas_call(
        kernel,
        name=name,
        out_shape=[jax.ShapeDtypeStruct(s, f32) for s in out_shapes],
        in_specs=specs,
        out_specs=out_specs or [VMEM] * len(out_shapes),
        scratch_shapes=list(scratch),
        compiler_params=pltpu.CompilerParams(vmem_limit_bytes=vmem * 1024 * 1024),
    )


def body(
    fluid_adjoint,
    fluid_rhs,
    diag_inverse,
    face_blocks,
    face_index,
    surface_cell,
    surface_count,
    transfer_node,
    transfer_weight,
    load_sens,
    disp_sens,
    struct_adjoint,
    struct_rhs,
    shell_blocks,
    shell_inverse,
    shell_columns,
):
    def shift(value, by):
        pairs = [(i, i + by) for i in range(DEVS) if 0 <= i + by < DEVS]
        return lax.ppermute(value, BOTH, pairs)

    sizes = [(NVAR, NVAR, FACES, CELL), (NVAR, NVAR, CELL), (NVAR, CELL), (NVAR, CELL),
             (NVAR, 3, SURF), (FACES, CELL), (TMAP, SURF), (TMAP, SURF), (1, SURF),
             (NVAR, 3, SURF)]
    kinds = [f32] * 5 + [jnp.int32] * 2 + [f32, jnp.int32, f32]
    own_shape = (2, G_ALL, 8, HALF)
    (own,) = call(
        pack_kernel, "pack", [own_shape], [ANY] * 10 + [SMEM],
        [pltpu.VMEM(s, k) for s, k in zip(sizes, kinds)]
        + [pltpu.VMEM(own_shape, f32), pltpu.SemaphoreType.DMA((10,)),
           pltpu.SemaphoreType.DMA((2,))],
        [ANY], vmem=63,
    )(face_blocks.transpose(1, 2, 0, 3), diag_inverse, fluid_rhs, fluid_adjoint,
      load_sens.transpose(1, 0, 2), face_index, transfer_node, transfer_weight,
      surface_cell.reshape(1, SURF), disp_sens, surface_count)
    rows = jnp.pad(struct_adjoint.reshape(2 * FLUID, BLK), ((0, 0), (0, LANES - BLK)))
    rows = jnp.broadcast_to(rows, (STRUCT,) + rows.shape)
    low = shift(own, 1)
    high = shift(own, -1)
    low_two = shift(own, 2)
    high_two = shift(own, -2)
    struct_rows = lax.all_to_all(rows, "struct", 0, 0, tiled=True).reshape(2 * DEVS, LANES)

    mine = 2 * lax.axis_index("fluid")
    take = lambda a, axis: lax.dynamic_slice_in_dim(a, mine, 2, axis)
    blocks = take(shell_blocks, 1).reshape(NB, 2, BLK, BLK)
    inverse = take(shell_inverse, 0).reshape(2, BLK, BLK)
    columns = take(shell_columns, 1)
    rhs_rows = take(struct_rhs.reshape(2 * FLUID, BLK), 0)

    packs = [own, low, high, low_two, high_two, shift(low[1], 2), shift(high[0], -2)]
    relay = ((lax.axis_index(BOTH)) // CHUNKS).astype(jnp.int32).reshape(1)

    def shell(struct_rows, start):
        (terms,) = call(
            functools.partial(shell_kernel, start), "shell", [(2, BLK)], [VMEM, VMEM, SMEM]
        )(struct_rows, blocks, columns)
        return terms

    def solve(shares, terms, shape, scratch):
        received = lax.all_to_all(shares, BOTH, 0, 0, tiled=True)
        (solved,) = call(solve_kernel, "solve", [shape], [VMEM] * 4 + [SMEM], scratch)(
            received, rhs_rows, terms, inverse, relay)
        return solved

    terms = shell(struct_rows, True)
    state, shares = fluid(True, packs, struct_rows)
    solved = solve(shares, terms, (4 * DEVS, LANES), [pltpu.VMEM((DEVS + 16, LANES), f32)])
    struct_rows = lax.all_to_all(solved, BOTH, 0, 0, tiled=True)
    terms = shell(struct_rows, False)
    state, shares = fluid(False, packs, struct_rows, state)
    solved = solve(shares, terms, (2 * FLUID, LANES), [])
    group = lax.all_to_all(solved, "fluid", 0, 0, tiled=True)
    return (state, group[:, 0:BLK].reshape(-1))


def solution(mesh):
    placed = (
        P(None, ("fluid", "struct")),
        P(None, ("fluid", "struct")),
        P(None, None, ("fluid", "struct")),
        P(None, None, None, ("fluid", "struct")),
        P(None, ("fluid", "struct")),
        P(("fluid", "struct")),
        P(("fluid", "struct")),
        P(None, ("fluid", "struct")),
        P(None, ("fluid", "struct")),
        P(None, None, ("fluid", "struct")),
        P(None, None, ("fluid", "struct")),
        P("struct"),
        P("struct"),
        P(None, "struct", None),
        P("struct", None),
        P(None, "struct"),
    )
    return jax.shard_map(
        body,
        mesh=mesh,
        in_specs=placed,
        out_specs=(P(None, ("fluid", "struct")), P("struct")),
        check_vma=False,
    )
```

```python
import functools

import jax
import jax.numpy as jnp
from jax import lax
from jax.experimental import pallas as pl
from jax.experimental.pallas import tpu as pltpu
from jax.sharding import PartitionSpec as P

NVAR = 5
FACES = 6
TMAP = 3
DOF = 6
BLK = 96
NB = 4
CELL = 512
HALF = 256
SURF = 256
LANES = 128
FLUID = 16
STRUCT = 8
DEVS = FLUID * STRUCT
PIECE_NODES = 32
PIECE = PIECE_NODES * 3
BOTH = ("fluid", "struct")
OFFSETS = (-3, -2, -1, 1, 2, 3)
CHUNKS = NVAR * CELL // LANES
SIDE = 5
G_FACE = 0
G_DIAG = 25
G_ALL = 30
R_PLACE = 0
R_RHS = 6
R_STATE = 11
R_OTHER = 16
R_NODE = 21
R_WEIGHT = 24
R_CELL = 27
R_LIVE = 28
R_DISP = 29
R_ALL = 2 * 25

f32 = jnp.float32
bf16 = jnp.bfloat16
NN = (((1,), (0,)), ((), ()))
NT = (((1,), (1,)), ((), ()))


def split(x):
    hi = x.astype(bf16)
    return hi, (x - hi.astype(f32)).astype(bf16)


def split3(x):
    hi = x.astype(bf16)
    rest = x - hi.astype(f32)
    mid = rest.astype(bf16)
    return hi, mid, (rest - mid.astype(f32)).astype(bf16)


def stack(x):
    return jnp.concatenate([x_half.astype(f32) for x_half in split(x)], axis=0).astype(bf16)


def fold(product):
    rows = product.shape[0] // 2
    return product[0:rows] + product[rows:2 * rows]


def dot(a, b, dims):
    return lax.dot_general(a, b, dims, preferred_element_type=f32)


def iota(shape, axis):
    return lax.broadcasted_iota(jnp.int32, shape, axis)


def one_hot(mask):
    return jnp.where(mask, f32(1.0), f32(0.0)).astype(bf16)


def component_perm(half):
    row, col = iota((PIECE, BLK), 0), iota((PIECE, BLK), 1)
    dof = col % DOF
    return one_hot((dof < 3) & (row == dof * PIECE_NODES + half * 16 + col // DOF))


def live_row(count):
    return jnp.where(iota((1, SURF), 1) < count, f32(1.0), f32(0.0))


def get_row(pack, at, lanes=slice(None)):
    return pack[at // 2, FACES + at % 2:FACES + at % 2 + 1, lanes]


def get_rows(pack, at, count, lanes=slice(None)):
    return jnp.concatenate([get_row(pack, at + i, lanes) for i in range(count)], axis=0)


def spread(part):
    return jnp.concatenate([part, jnp.zeros((part.shape[0], LANES - part.shape[1]), f32)], axis=1)


def components(parts):
    total = None
    for half, part in enumerate(parts):
        perm = component_perm(half)
        for term in split3(part):
            product = dot(term, perm, NT)
            total = product if total is None else total + product
    return total


def by_device(node):
    return ((node >> 5) & 15) * STRUCT + (node >> 9)


def by_piece(node):
    return node >> 5


def start_copies(pairs, sems):
    copies = [pltpu.make_async_copy(s, d, sems.at[i]) for i, (s, d) in enumerate(pairs)]
    for copy in copies:
        copy.start()
    return copies


def pack_kernel(face, diag, rhs, state, load, place, node, weight, cell, disp, count,
                own,
                face_v, diag_v, rhs_v, state_v, load_v, place_v, node_v, weight_v, cell_v,
                disp_v, own_v, sems, out_sems):
    copies = start_copies(
        [(face, face_v), (diag, diag_v), (rhs, rhs_v), (state, state_v), (load, load_v),
         (place, place_v), (node, node_v), (weight, weight_v), (cell, cell_v),
         (disp, disp_v)], sems)
    for copy in copies:
        copy.wait()
    live = live_row(count[0])
    sent = []
    for half in range(2):
        cols = slice(half * HALF, (half + 1) * HALF)
        other = slice((1 - half) * HALF, (2 - half) * HALF)
        pack = own_v.at[half]

        def put(at, value):
            pack[at // 2, FACES + at % 2:FACES + at % 2 + 1, :] = value

        for u in range(NVAR):
            for v in range(NVAR):
                pack[G_FACE + u * NVAR + v, 0:FACES, :] = face_v[u, v, :, cols]
                pack[G_DIAG + u, v:v + 1, :] = diag_v[v, u:u + 1, cols]
            pack[G_DIAG + u, 5:8, :] = load_v[u]
        shift = iota((1, HALF), 1) // LANES * LANES + half * HALF
        for k in range(FACES):
            put(R_PLACE + k, (place_v[k:k + 1, cols] - shift).astype(f32))
        for v in range(NVAR):
            put(R_RHS + v, rhs_v[v:v + 1, cols])
            put(R_STATE + v, state_v[v:v + 1, cols])
            put(R_OTHER + v, state_v[v:v + 1, other])
        for t in range(TMAP):
            put(R_NODE + t, node_v[t:t + 1, :].astype(f32))
            put(R_WEIGHT + t, weight_v[t:t + 1, :])
        put(R_CELL, cell_v[...].astype(f32))
        put(R_LIVE, live)
        for v in range(NVAR):
            for j in range(3):
                put(R_DISP + 3 * v + j, disp_v[v, j:j + 1, :])
        for at in range(R_DISP + 3 * NVAR, R_ALL):
            put(at, jnp.zeros((1, HALF), f32))
        sent.append(pltpu.make_async_copy(own_v.at[half], own.at[half], out_sems.at[half]))
        sent[-1].start()
    for copy in sent:
        copy.wait()


def slots(pack):
    node = get_rows(pack, R_NODE, TMAP).astype(jnp.int32)
    weight = get_rows(pack, R_WEIGHT, TMAP)
    cell = get_row(pack, R_CELL).astype(jnp.int32)
    live = get_row(pack, R_LIVE)
    return node, weight, cell, live


def surface_loads(struct_t, pack, row_of):
    node, weight, cell, live = slots(pack)
    total = [None] * 3
    for t in range(TMAP):
        nodes = node[t:t + 1, :]
        pick = one_hot(iota((DEVS, SURF), 0) == row_of(nodes))
        found = fold(dot(struct_t, pick, NN))
        gain = jnp.where(iota((PIECE_NODES, SURF), 0) == (nodes & 31), weight[t:t + 1, :], f32(0.0))
        for j in range(3):
            term = found[j * PIECE_NODES:(j + 1) * PIECE_NODES] * gain
            total[j] = term if total[j] is None else total[j] + term
    moved = [jnp.sum(x, axis=0, keepdims=True) * live for x in total]
    shown = []
    for v in range(NVAR):
        term = None
        for j in range(3):
            part = pack[G_DIAG + v, 5 + j:6 + j, :] * moved[j]
            term = part if term is None else term + part
        shown.append(term)
    shown.append(jnp.zeros((8 - NVAR, SURF), f32))
    return stack(jnp.concatenate(shown, axis=0))


def fluid_kernel(start, *refs):
    refs = list(refs)
    take = lambda n: [refs.pop(0) for _ in range(n)]
    pack_refs = take(len(PACKS))
    (struct_v,) = take(1)
    if not start:
        (state_v,) = take(1)
    out, shares = take(2)
    x0, x1, source, places, chunks = take(5)

    side = SIDE
    packs = {}
    for ref, (at, count) in zip(pack_refs, PACKS):
        for i in range(count):
            packs[side + at + i] = ref.at[i] if count > 1 else ref

    base = 2 * (side + 1)
    if not start:
        chunks[...] = struct_v[pl.ds(3, DEVS, stride=4), :]
        for c in range(4):
            x0[base + c, 0:NVAR, :] = state_v[:, c * LANES:(c + 1) * LANES]
            for k, offset in enumerate(OFFSETS):
                row = k * CHUNKS + c * NVAR
                x0[base + 4 * offset + c, 0:NVAR, :] = chunks[row:row + NVAR, :]

    if start:
        parts = [struct_v[pl.ds(half, DEVS, stride=2), :][:, 0:BLK] for half in range(2)]
        struct_t = stack(jnp.transpose(spread(components(parts))))
    else:
        struct_t = stack(jnp.transpose(struct_v[pl.ds(2, DEVS, stride=4), :]))
    row_of = by_piece if start else by_device
    for which, (begin, count) in enumerate(PACKS):
        present = list(range(begin, begin + count))
        pack = packs[side + present[0]]
        loads = surface_loads(struct_t, pack, row_of)
        cell = get_row(pack, R_CELL).astype(jnp.int32)
        for h in present:
            at = one_hot(iota((HALF, SURF), 0) + (h % 2) * HALF == cell)
            coupled = fold(dot(loads, at, NT))
            value = coupled[0:NVAR] + get_rows(packs[side + h], R_RHS, NVAR)
            place = get_rows(packs[side + h], R_PLACE, FACES).astype(jnp.int32)
            for c in range(2):
                lanes = slice(c * LANES, (c + 1) * LANES)
                chunk = 2 * (side + h) + c
                source[chunk, 0:NVAR, :] = value[:, lanes]
                places[chunk, 0:FACES, :] = place[:, lanes]
                places[chunk, FACES:8, :] = jnp.full((8 - FACES, LANES), -1, jnp.int32)
            if start:
                wanted = [(h, R_STATE)]
                wanted += [(h - 1, R_OTHER)] * (h == -side)
                wanted += [(h + 1, R_OTHER)] * (h == side + 1)
                for to, row in wanted:
                    lines = get_rows(packs[side + h], row, NVAR)
                    for c in range(2):
                        x0[base + 2 * to + c, 0:NVAR, :] = lines[:, c * LANES:(c + 1) * LANES]

    def sweep_half(x_in, x_out, half, write):
        for c in range(2):
            lanes = slice(c * LANES, (c + 1) * LANES)
            chunk = 2 * half + c
            place = places[chunk]
            lane_of, chunk_of = place & (LANES - 1), place >> 7
            masks = [chunk_of == o for o in range(5)]
            sums = [None] * NVAR
            for u in range(NVAR):
                near = None
                for o in range(5):
                    row = jnp.broadcast_to(x_in[chunk + o, u:u + 1, :], (8, LANES))
                    found = jnp.take_along_axis(row, lane_of, axis=1, mode="promise_in_bounds")
                    near = jnp.where(masks[o], found, f32(0.0) if o == 0 else near)
                for v in range(NVAR):
                    term = packs[half][G_FACE + u * NVAR + v, :, lanes] * near
                    sums[v] = term if sums[v] is None else sums[v] + term
            new = None
            for u in range(NVAR):
                left = source[chunk, u:u + 1, :] - jnp.sum(sums[u], axis=0, keepdims=True)
                term = packs[half][G_DIAG + u, 0:NVAR, lanes] * left
                new = term if new is None else new + term
            write(chunk, new)

    x_in, x_out = x0, x1
    for step in range(SIDE + 1):
        reach = SIDE - step
        done = step == SIDE
        if done:
            def write(chunk, new):
                at = (chunk - 2 * side) * LANES
                out[:, at:at + LANES] = new
        else:
            def write(chunk, new, x_out=x_out):
                x_out[chunk + 2, 0:NVAR, :] = new
        first, end = side - reach, side + 2 + reach
        for half in range(first, end):
            sweep_half(x_in, x_out, half, write)
        x_in, x_out = x_out, x_in

    node, weight, cell, live = slots(packs[side])
    at = one_hot(iota((CELL, SURF), 0) == cell)
    state = jnp.concatenate([out[...], jnp.zeros((8 - NVAR, CELL), f32)], axis=0)
    surface = fold(dot(stack(state), at, NN))
    sens = None
    for v in range(NVAR):
        term = get_rows(packs[side], R_DISP + 3 * v, 3) * surface[v:v + 1, :]
        sens = term if sens is None else sens + term
    sens = sens * live
    total = None
    for t in range(TMAP):
        nodes = node[t:t + 1, :]
        pick = one_hot(iota((DEVS, SURF), 0) == by_device(nodes))
        gain = jnp.where(iota((PIECE_NODES, SURF), 0) == (nodes & 31),
                         weight[t:t + 1, :], f32(0.0))
        value = jnp.concatenate([gain * sens[j:j + 1, :] for j in range(3)], axis=0)
        term = dot(pick, stack(value), NT)
        total = term if total is None else total + term
    wide = spread(total[:, 0:PIECE] + total[:, PIECE:2 * PIECE])
    if not start:
        shares[...] = wide
    else:
        shares[pl.ds(0, DEVS, stride=2), :] = wide
        for k in range(len(OFFSETS)):
            for c in range(4):
                row = k * CHUNKS + c * NVAR
                chunks[row:row + NVAR, :] = out[:, c * LANES:(c + 1) * LANES]
        rest = len(OFFSETS) * CHUNKS
        chunks[rest:DEVS, :] = jnp.zeros((DEVS - rest, LANES), f32)
        shares[pl.ds(1, DEVS, stride=2), :] = chunks[...]


PACKS = ((0, 2), (-4, 2), (4, 2), (-2, 2), (2, 2), (-5, 1), (6, 1))


def fluid(start, packs, struct_rows, state=None):
    args = list(packs) + [struct_rows] + ([] if start else [state])
    halves = 2 * SIDE + 2
    scratch = [
        pltpu.VMEM((2 * halves + 4, 8, LANES), f32),
        pltpu.VMEM((2 * halves + 4, 8, LANES), f32),
        pltpu.VMEM((2 * halves, 8, LANES), f32),
        pltpu.VMEM((2 * halves, 8, LANES), jnp.int32),
        pltpu.VMEM((DEVS, LANES), f32),
    ]
    outs = [(NVAR, CELL), (2 * DEVS if start else DEVS, LANES)]
    return call(functools.partial(fluid_kernel, start), "fluid", outs, [VMEM] * len(args), scratch)(*args)


def shell_kernel(whole_rows, struct_rows, blocks, columns, out):
    for half in range(2):
        total = jnp.zeros((1, BLK), f32)
        for m in range(NB):
            column = columns[m, half]
            piece = column // 2
            row = (piece % FLUID) * STRUCT + piece // FLUID
            line = column if whole_rows else 4 * row + column % 2
            x = struct_rows[pl.ds(line, 1), :][:, 0:BLK]
            x_hi, x_lo = split(x)
            b_hi, b_lo = split(blocks[m, half])
            total += dot(x_hi, b_hi, NN) + dot(x_lo, b_hi, NN) + dot(x_hi, b_lo, NN)
        out[half:half + 1, :] = total


def solve_kernel(received, rhs, shell, inverse, relay, out, *padded):
    start = bool(padded)
    lines = received[pl.ds(0, DEVS, stride=2), :] if start else received[...]
    parts = split3(jnp.sum(lines, axis=0, keepdims=True)[:, 0:PIECE])
    new = []
    for half in range(2):
        perm = component_perm(half)
        load = dot(parts[0], perm, NN) + dot(parts[1], perm, NN) + dot(parts[2], perm, NN)
        right = rhs[half:half + 1, :] + load - shell[half:half + 1, :]
        r_hi, r_lo = split(right)
        i_hi, i_lo = split(inverse[half])
        new.append(dot(r_hi, i_hi, NT) + dot(r_lo, i_hi, NT) + dot(r_hi, i_lo, NT))
    rows = new + [components(new)] if start else new
    every = 4 if start else 2
    count = out.shape[0] // every
    for j, part in enumerate(rows):
        out[pl.ds(j, count, stride=every), :] = jnp.broadcast_to(spread(part), (count, LANES))
    if start:
        (lined,) = padded
        lined[0:8, :] = jnp.zeros((8, LANES), f32)
        lined[8:8 + DEVS, :] = received[pl.ds(1, DEVS, stride=2), :]
        lined[8 + DEVS:16 + DEVS, :] = jnp.zeros((8, LANES), f32)
        for k, offset in enumerate(OFFSETS):
            @pl.when(relay[0] == k)
            def _():
                out[pl.ds(3, DEVS, stride=4), :] = lined[8 + offset:8 + offset + DEVS, :]

        @pl.when(relay[0] >= len(OFFSETS))
        def _():
            out[pl.ds(3, DEVS, stride=4), :] = jnp.zeros((DEVS, LANES), f32)


VMEM = pl.BlockSpec(memory_space=pltpu.VMEM)
SMEM = pl.BlockSpec(memory_space=pltpu.SMEM)
ANY = pl.BlockSpec(memory_space=pltpu.HBM)


def call(kernel, name, out_shapes, specs, scratch=(), out_specs=None, vmem=16):
    return pl.pallas_call(
        kernel,
        name=name,
        out_shape=[jax.ShapeDtypeStruct(s, f32) for s in out_shapes],
        in_specs=specs,
        out_specs=out_specs or [VMEM] * len(out_shapes),
        scratch_shapes=list(scratch),
        compiler_params=pltpu.CompilerParams(vmem_limit_bytes=vmem * 1024 * 1024),
    )


def body(
    fluid_adjoint,
    fluid_rhs,
    diag_inverse,
    face_blocks,
    face_index,
    surface_cell,
    surface_count,
    transfer_node,
    transfer_weight,
    load_sens,
    disp_sens,
    struct_adjoint,
    struct_rhs,
    shell_blocks,
    shell_inverse,
    shell_columns,
):
    def shift(value, by):
        pairs = [(i, i + by) for i in range(DEVS) if 0 <= i + by < DEVS]
        return lax.ppermute(value, BOTH, pairs)

    sizes = [(NVAR, NVAR, FACES, CELL), (NVAR, NVAR, CELL), (NVAR, CELL), (NVAR, CELL),
             (NVAR, 3, SURF), (FACES, CELL), (TMAP, SURF), (TMAP, SURF), (1, SURF),
             (NVAR, 3, SURF)]
    kinds = [f32] * 5 + [jnp.int32] * 2 + [f32, jnp.int32, f32]
    own_shape = (2, G_ALL, 8, HALF)
    (own,) = call(
        pack_kernel, "pack", [own_shape], [ANY] * 10 + [SMEM],
        [pltpu.VMEM(s, k) for s, k in zip(sizes, kinds)]
        + [pltpu.VMEM(own_shape, f32), pltpu.SemaphoreType.DMA((10,)),
           pltpu.SemaphoreType.DMA((2,))],
        [ANY], vmem=63,
    )(face_blocks.transpose(1, 2, 0, 3), diag_inverse, fluid_rhs, fluid_adjoint,
      load_sens.transpose(1, 0, 2), face_index, transfer_node, transfer_weight,
      surface_cell.reshape(1, SURF), disp_sens, surface_count)
    rows = jnp.pad(struct_adjoint.reshape(2 * FLUID, BLK), ((0, 0), (0, LANES - BLK)))
    rows = jnp.broadcast_to(rows, (STRUCT,) + rows.shape)
    low = shift(own, 1)
    high = shift(own, -1)
    low_two = shift(own, 2)
    high_two = shift(own, -2)
    struct_rows = lax.all_to_all(rows, "struct", 0, 0, tiled=True).reshape(2 * DEVS, LANES)

    mine = 2 * lax.axis_index("fluid")
    take = lambda a, axis: lax.dynamic_slice_in_dim(a, mine, 2, axis)
    blocks = take(shell_blocks, 1).reshape(NB, 2, BLK, BLK)
    inverse = take(shell_inverse, 0).reshape(2, BLK, BLK)
    columns = take(shell_columns, 1)
    rhs_rows = take(struct_rhs.reshape(2 * FLUID, BLK), 0)

    packs = [own, low_two, high_two, low, high, shift(low[1], 2), shift(high[0], -2)]
    relay = ((lax.axis_index(BOTH)) // CHUNKS).astype(jnp.int32).reshape(1)

    def shell(struct_rows, start):
        (terms,) = call(
            functools.partial(shell_kernel, start), "shell", [(2, BLK)], [VMEM, VMEM, SMEM]
        )(struct_rows, blocks, columns)
        return terms

    def solve(shares, terms, shape, scratch):
        received = lax.all_to_all(shares, BOTH, 0, 0, tiled=True)
        (solved,) = call(solve_kernel, "solve", [shape], [VMEM] * 4 + [SMEM], scratch)(
            received, rhs_rows, terms, inverse, relay)
        return solved

    terms = shell(struct_rows, True)
    state, shares = fluid(True, packs, struct_rows)
    solved = solve(shares, terms, (4 * DEVS, LANES), [pltpu.VMEM((DEVS + 16, LANES), f32)])
    struct_rows = lax.all_to_all(solved, BOTH, 0, 0, tiled=True)
    terms = shell(struct_rows, False)
    state, shares = fluid(False, packs, struct_rows, state)
    solved = solve(shares, terms, (2 * FLUID, LANES), [])
    group = lax.all_to_all(solved, "fluid", 0, 0, tiled=True)
    return (state, group[:, 0:BLK].reshape(-1))


def solution(mesh):
    placed = (
        P(None, ("fluid", "struct")),
        P(None, ("fluid", "struct")),
        P(None, None, ("fluid", "struct")),
        P(None, None, None, ("fluid", "struct")),
        P(None, ("fluid", "struct")),
        P(("fluid", "struct")),
        P(("fluid", "struct")),
        P(None, ("fluid", "struct")),
        P(None, ("fluid", "struct")),
        P(None, None, ("fluid", "struct")),
        P(None, None, ("fluid", "struct")),
        P("struct"),
        P("struct"),
        P(None, "struct", None),
        P("struct", None),
        P(None, "struct"),
    )
    return jax.shard_map(
        body,
        mesh=mesh,
        in_specs=placed,
        out_specs=(P(None, ("fluid", "struct")), P("struct")),
        check_vma=False,
    )
```

```python
import functools

import jax
import jax.numpy as jnp
from jax import lax
from jax.experimental import pallas as pl
from jax.experimental.pallas import tpu as pltpu
from jax.sharding import PartitionSpec as P

NVAR = 5
FACES = 6
TMAP = 3
DOF = 6
BLK = 96
NB = 4
CELL = 512
HALF = 256
SURF = 256
LANES = 128
FLUID = 16
STRUCT = 8
DEVS = FLUID * STRUCT
PIECE_NODES = 32
PIECE = PIECE_NODES * 3
BOTH = ("fluid", "struct")
OFFSETS = (-3, -2, -1, 1, 2, 3)
CHUNKS = NVAR * CELL // LANES
SIDE = 5
G_FACE = 0
G_DIAG = 25
G_ALL = 30
R_PLACE = 0
R_RHS = 6
R_STATE = 11
R_OTHER = 16
R_NODE = 21
R_WEIGHT = 24
R_CELL = 27
R_LIVE = 28
R_DISP = 29
R_ALL = 2 * 25

f32 = jnp.float32
bf16 = jnp.bfloat16
NN = (((1,), (0,)), ((), ()))
NT = (((1,), (1,)), ((), ()))


def split(x):
    hi = x.astype(bf16)
    return hi, (x - hi.astype(f32)).astype(bf16)


def split3(x):
    hi = x.astype(bf16)
    rest = x - hi.astype(f32)
    mid = rest.astype(bf16)
    return hi, mid, (rest - mid.astype(f32)).astype(bf16)


def stack(x):
    return jnp.concatenate([x_half.astype(f32) for x_half in split(x)], axis=0).astype(bf16)


def fold(product):
    rows = product.shape[0] // 2
    return product[0:rows] + product[rows:2 * rows]


def dot(a, b, dims):
    return lax.dot_general(a, b, dims, preferred_element_type=f32)


def iota(shape, axis):
    return lax.broadcasted_iota(jnp.int32, shape, axis)


def one_hot(mask):
    return jnp.where(mask, f32(1.0), f32(0.0)).astype(bf16)


def component_perm(half):
    row, col = iota((PIECE, BLK), 0), iota((PIECE, BLK), 1)
    dof = col % DOF
    return one_hot((dof < 3) & (row == dof * PIECE_NODES + half * 16 + col // DOF))


def live_row(count):
    return jnp.where(iota((1, SURF), 1) < count, f32(1.0), f32(0.0))


def get_row(pack, at, lanes=slice(None)):
    return pack[at // 2, FACES + at % 2:FACES + at % 2 + 1, lanes]


def get_rows(pack, at, count, lanes=slice(None)):
    return jnp.concatenate([get_row(pack, at + i, lanes) for i in range(count)], axis=0)


def spread(part):
    return jnp.concatenate([part, jnp.zeros((part.shape[0], LANES - part.shape[1]), f32)], axis=1)


def components(parts):
    total = None
    for half, part in enumerate(parts):
        perm = component_perm(half)
        for term in split3(part):
            product = dot(term, perm, NT)
            total = product if total is None else total + product
    return total


def by_device(node):
    return ((node >> 5) & 15) * STRUCT + (node >> 9)


def by_piece(node):
    return node >> 5


def start_copies(pairs, sems):
    copies = [pltpu.make_async_copy(s, d, sems.at[i]) for i, (s, d) in enumerate(pairs)]
    for copy in copies:
        copy.start()
    return copies


def pack_kernel(face, diag, rhs, state, load, place, node, weight, cell, disp, count,
                own,
                face_v, diag_v, rhs_v, state_v, load_v, place_v, node_v, weight_v, cell_v,
                disp_v, own_v, sems, out_sems):
    copies = start_copies(
        [(face, face_v), (diag, diag_v), (rhs, rhs_v), (state, state_v), (load, load_v),
         (place, place_v), (node, node_v), (weight, weight_v), (cell, cell_v),
         (disp, disp_v)], sems)
    for copy in copies:
        copy.wait()
    live = live_row(count[0])
    sent = []
    for half in range(2):
        cols = slice(half * HALF, (half + 1) * HALF)
        other = slice((1 - half) * HALF, (2 - half) * HALF)
        pack = own_v.at[half]

        def put(at, value):
            pack[at // 2, FACES + at % 2:FACES + at % 2 + 1, :] = value

        for u in range(NVAR):
            for v in range(NVAR):
                pack[G_FACE + u * NVAR + v, 0:FACES, :] = face_v[u, v, :, cols]
                pack[G_DIAG + u, v:v + 1, :] = diag_v[v, u:u + 1, cols]
            pack[G_DIAG + u, 5:8, :] = load_v[u]
        shift = iota((1, HALF), 1) // LANES * LANES + half * HALF
        for k in range(FACES):
            put(R_PLACE + k, (place_v[k:k + 1, cols] - shift).astype(f32))
        for v in range(NVAR):
            put(R_RHS + v, rhs_v[v:v + 1, cols])
            put(R_STATE + v, state_v[v:v + 1, cols])
            put(R_OTHER + v, state_v[v:v + 1, other])
        for t in range(TMAP):
            put(R_NODE + t, node_v[t:t + 1, :].astype(f32))
            put(R_WEIGHT + t, weight_v[t:t + 1, :])
        put(R_CELL, cell_v[...].astype(f32))
        put(R_LIVE, live)
        for v in range(NVAR):
            for j in range(3):
                put(R_DISP + 3 * v + j, disp_v[v, j:j + 1, :])
        for at in range(R_DISP + 3 * NVAR, R_ALL):
            put(at, jnp.zeros((1, HALF), f32))
        sent.append(pltpu.make_async_copy(own_v.at[half], own.at[half], out_sems.at[half]))
        sent[-1].start()
    for copy in sent:
        copy.wait()


def slots(pack):
    node = get_rows(pack, R_NODE, TMAP).astype(jnp.int32)
    weight = get_rows(pack, R_WEIGHT, TMAP)
    cell = get_row(pack, R_CELL).astype(jnp.int32)
    live = get_row(pack, R_LIVE)
    return node, weight, cell, live


def surface_loads(struct_t, pack, row_of):
    node, weight, cell, live = slots(pack)
    total = [None] * 3
    for t in range(TMAP):
        nodes = node[t:t + 1, :]
        pick = one_hot(iota((DEVS, SURF), 0) == row_of(nodes))
        found = fold(dot(struct_t, pick, NN))
        gain = jnp.where(iota((PIECE_NODES, SURF), 0) == (nodes & 31), weight[t:t + 1, :], f32(0.0))
        for j in range(3):
            term = found[j * PIECE_NODES:(j + 1) * PIECE_NODES] * gain
            total[j] = term if total[j] is None else total[j] + term
    moved = [jnp.sum(x, axis=0, keepdims=True) * live for x in total]
    shown = []
    for v in range(NVAR):
        term = None
        for j in range(3):
            part = pack[G_DIAG + v, 5 + j:6 + j, :] * moved[j]
            term = part if term is None else term + part
        shown.append(term)
    shown.append(jnp.zeros((8 - NVAR, SURF), f32))
    return stack(jnp.concatenate(shown, axis=0))


def fluid_kernel(start, *refs):
    refs = list(refs)
    take = lambda n: [refs.pop(0) for _ in range(n)]
    pack_refs = take(len(PACKS))
    (struct_v,) = take(1)
    if not start:
        (state_v,) = take(1)
    out, shares = take(2)
    x0, x1, source, places, chunks = take(5)

    side = SIDE
    packs = {}
    for ref, (at, count) in zip(pack_refs, PACKS):
        for i in range(count):
            packs[side + at + i] = ref.at[i] if count > 1 else ref

    base = 2 * (side + 1)
    if not start:
        chunks[...] = struct_v[pl.ds(3, DEVS, stride=4), :]
        for c in range(4):
            x0[base + c, 0:NVAR, :] = state_v[:, c * LANES:(c + 1) * LANES]
            for k, offset in enumerate(OFFSETS):
                row = k * CHUNKS + c * NVAR
                x0[base + 4 * offset + c, 0:NVAR, :] = chunks[row:row + NVAR, :]

    if start:
        parts = [struct_v[pl.ds(half, DEVS, stride=2), :][:, 0:BLK] for half in range(2)]
        struct_t = stack(jnp.transpose(spread(components(parts))))
    else:
        struct_t = stack(jnp.transpose(struct_v[pl.ds(2, DEVS, stride=4), :]))
    row_of = by_piece if start else by_device
    for which, (begin, count) in enumerate(PACKS):
        present = list(range(begin, begin + count))
        pack = packs[side + present[0]]
        loads = surface_loads(struct_t, pack, row_of)
        cell = get_row(pack, R_CELL).astype(jnp.int32)
        for h in present:
            at = one_hot(iota((HALF, SURF), 0) + (h % 2) * HALF == cell)
            coupled = fold(dot(loads, at, NT))
            value = coupled[0:NVAR] + get_rows(packs[side + h], R_RHS, NVAR)
            place = get_rows(packs[side + h], R_PLACE, FACES).astype(jnp.int32)
            for c in range(2):
                lanes = slice(c * LANES, (c + 1) * LANES)
                chunk = 2 * (side + h) + c
                source[chunk, 0:NVAR, :] = value[:, lanes]
                places[chunk, 0:FACES, :] = place[:, lanes]
                places[chunk, FACES:8, :] = jnp.full((8 - FACES, LANES), -1, jnp.int32)
            if start:
                wanted = [(h, R_STATE)]
                wanted += [(h - 1, R_OTHER)] * (h == -side)
                wanted += [(h + 1, R_OTHER)] * (h == side + 1)
                for to, row in wanted:
                    lines = get_rows(packs[side + h], row, NVAR)
                    for c in range(2):
                        x0[base + 2 * to + c, 0:NVAR, :] = lines[:, c * LANES:(c + 1) * LANES]

    def sweep_half(x_in, x_out, half, write):
        for c in range(2):
            lanes = slice(c * LANES, (c + 1) * LANES)
            chunk = 2 * half + c
            place = places[chunk]
            lane_of, chunk_of = place & (LANES - 1), place >> 7
            masks = [chunk_of == o for o in range(5)]
            sums = [None] * NVAR
            for u in range(NVAR):
                near = None
                for o in range(5):
                    row = jnp.broadcast_to(x_in[chunk + o, u:u + 1, :], (8, LANES))
                    found = jnp.take_along_axis(row, lane_of, axis=1, mode="promise_in_bounds")
                    near = jnp.where(masks[o], found, f32(0.0) if o == 0 else near)
                for v in range(NVAR):
                    term = packs[half][G_FACE + u * NVAR + v, :, lanes] * near
                    sums[v] = term if sums[v] is None else sums[v] + term
            new = None
            for u in range(NVAR):
                left = source[chunk, u:u + 1, :] - jnp.sum(sums[u], axis=0, keepdims=True)
                term = packs[half][G_DIAG + u, 0:NVAR, lanes] * left
                new = term if new is None else new + term
            write(chunk, new)

    x_in, x_out = x0, x1
    for step in range(SIDE + 1):
        reach = SIDE - step
        done = step == SIDE
        if done:
            def write(chunk, new):
                at = (chunk - 2 * side) * LANES
                out[:, at:at + LANES] = new
        else:
            def write(chunk, new, x_out=x_out):
                x_out[chunk + 2, 0:NVAR, :] = new
        first, end = side - reach, side + 2 + reach
        for half in range(first, end):
            sweep_half(x_in, x_out, half, write)
        x_in, x_out = x_out, x_in

    node, weight, cell, live = slots(packs[side])
    at = one_hot(iota((CELL, SURF), 0) == cell)
    state = jnp.concatenate([out[...], jnp.zeros((8 - NVAR, CELL), f32)], axis=0)
    surface = fold(dot(stack(state), at, NN))
    sens = None
    for v in range(NVAR):
        term = get_rows(packs[side], R_DISP + 3 * v, 3) * surface[v:v + 1, :]
        sens = term if sens is None else sens + term
    sens = sens * live
    total = None
    for t in range(TMAP):
        nodes = node[t:t + 1, :]
        pick = one_hot(iota((DEVS, SURF), 0) == by_device(nodes))
        gain = jnp.where(iota((PIECE_NODES, SURF), 0) == (nodes & 31),
                         weight[t:t + 1, :], f32(0.0))
        value = jnp.concatenate([gain * sens[j:j + 1, :] for j in range(3)], axis=0)
        term = dot(pick, stack(value), NT)
        total = term if total is None else total + term
    wide = spread(total[:, 0:PIECE] + total[:, PIECE:2 * PIECE])
    if not start:
        shares[...] = wide
    else:
        shares[pl.ds(0, DEVS, stride=2), :] = wide
        for k in range(len(OFFSETS)):
            for c in range(4):
                row = k * CHUNKS + c * NVAR
                chunks[row:row + NVAR, :] = out[:, c * LANES:(c + 1) * LANES]
        rest = len(OFFSETS) * CHUNKS
        chunks[rest:DEVS, :] = jnp.zeros((DEVS - rest, LANES), f32)
        shares[pl.ds(1, DEVS, stride=2), :] = chunks[...]


PACKS = ((0, 2), (-4, 2), (4, 2), (-2, 2), (2, 2), (-5, 1), (6, 1))


def fluid(start, packs, struct_rows, state=None):
    args = list(packs) + [struct_rows] + ([] if start else [state])
    halves = 2 * SIDE + 2
    scratch = [
        pltpu.VMEM((2 * halves + 4, 8, LANES), f32),
        pltpu.VMEM((2 * halves + 4, 8, LANES), f32),
        pltpu.VMEM((2 * halves, 8, LANES), f32),
        pltpu.VMEM((2 * halves, 8, LANES), jnp.int32),
        pltpu.VMEM((DEVS, LANES), f32),
    ]
    outs = [(NVAR, CELL), (2 * DEVS if start else DEVS, LANES)]
    return call(functools.partial(fluid_kernel, start), "fluid", outs, [VMEM] * len(args), scratch)(*args)


def shell_kernel(whole_rows, struct_rows, blocks, columns, out):
    for half in range(2):
        total = jnp.zeros((1, BLK), f32)
        for m in range(NB):
            column = columns[m, half]
            piece = column // 2
            row = (piece % FLUID) * STRUCT + piece // FLUID
            line = column if whole_rows else 4 * row + column % 2
            x = struct_rows[pl.ds(line, 1), :][:, 0:BLK]
            x_hi, x_lo = split(x)
            b_hi, b_lo = split(blocks[m, half])
            total += dot(x_hi, b_hi, NN) + dot(x_lo, b_hi, NN) + dot(x_hi, b_lo, NN)
        out[half:half + 1, :] = total


def solve_kernel(held, received, rhs, shell, inverse, relay, *refs):
    out, *padded = refs[held:]
    start = bool(padded)
    lines = received[pl.ds(0, DEVS, stride=2), :] if start else received[...]
    parts = split3(jnp.sum(lines, axis=0, keepdims=True)[:, 0:PIECE])
    new = []
    for half in range(2):
        perm = component_perm(half)
        load = dot(parts[0], perm, NN) + dot(parts[1], perm, NN) + dot(parts[2], perm, NN)
        right = rhs[half:half + 1, :] + load - shell[half:half + 1, :]
        r_hi, r_lo = split(right)
        i_hi, i_lo = split(inverse[half])
        new.append(dot(r_hi, i_hi, NT) + dot(r_lo, i_hi, NT) + dot(r_hi, i_lo, NT))
    rows = new + [components(new)] if start else new
    every = 4 if start else 2
    count = out.shape[0] // every
    for j, part in enumerate(rows):
        out[pl.ds(j, count, stride=every), :] = jnp.broadcast_to(spread(part), (count, LANES))
    if start:
        (lined,) = padded
        lined[0:8, :] = jnp.zeros((8, LANES), f32)
        lined[8:8 + DEVS, :] = received[pl.ds(1, DEVS, stride=2), :]
        lined[8 + DEVS:16 + DEVS, :] = jnp.zeros((8, LANES), f32)
        for k, offset in enumerate(OFFSETS):
            @pl.when(relay[0] == k)
            def _():
                out[pl.ds(3, DEVS, stride=4), :] = lined[8 + offset:8 + offset + DEVS, :]

        @pl.when(relay[0] >= len(OFFSETS))
        def _():
            out[pl.ds(3, DEVS, stride=4), :] = jnp.zeros((DEVS, LANES), f32)


VMEM = pl.BlockSpec(memory_space=pltpu.VMEM)
SMEM = pl.BlockSpec(memory_space=pltpu.SMEM)
ANY = pl.BlockSpec(memory_space=pltpu.HBM)


def call(kernel, name, out_shapes, specs, scratch=(), out_specs=None, vmem=16):
    return pl.pallas_call(
        kernel,
        name=name,
        out_shape=[jax.ShapeDtypeStruct(s, f32) for s in out_shapes],
        in_specs=specs,
        out_specs=out_specs or [VMEM] * len(out_shapes),
        scratch_shapes=list(scratch),
        compiler_params=pltpu.CompilerParams(vmem_limit_bytes=vmem * 1024 * 1024),
    )


def body(
    fluid_adjoint,
    fluid_rhs,
    diag_inverse,
    face_blocks,
    face_index,
    surface_cell,
    surface_count,
    transfer_node,
    transfer_weight,
    load_sens,
    disp_sens,
    struct_adjoint,
    struct_rhs,
    shell_blocks,
    shell_inverse,
    shell_columns,
):
    def shift(value, by):
        pairs = [(i, i + by) for i in range(DEVS) if 0 <= i + by < DEVS]
        return lax.ppermute(value, BOTH, pairs)

    sizes = [(NVAR, NVAR, FACES, CELL), (NVAR, NVAR, CELL), (NVAR, CELL), (NVAR, CELL),
             (NVAR, 3, SURF), (FACES, CELL), (TMAP, SURF), (TMAP, SURF), (1, SURF),
             (NVAR, 3, SURF)]
    kinds = [f32] * 5 + [jnp.int32] * 2 + [f32, jnp.int32, f32]
    own_shape = (2, G_ALL, 8, HALF)
    (own,) = call(
        pack_kernel, "pack", [own_shape], [ANY] * 10 + [SMEM],
        [pltpu.VMEM(s, k) for s, k in zip(sizes, kinds)]
        + [pltpu.VMEM(own_shape, f32), pltpu.SemaphoreType.DMA((10,)),
           pltpu.SemaphoreType.DMA((2,))],
        [ANY], vmem=63,
    )(face_blocks.transpose(1, 2, 0, 3), diag_inverse, fluid_rhs, fluid_adjoint,
      load_sens.transpose(1, 0, 2), face_index, transfer_node, transfer_weight,
      surface_cell.reshape(1, SURF), disp_sens, surface_count)
    rows = jnp.pad(struct_adjoint.reshape(2 * FLUID, BLK), ((0, 0), (0, LANES - BLK)))
    rows = jnp.broadcast_to(rows, (STRUCT,) + rows.shape)
    low = shift(own, 1)
    high = shift(own, -1)
    low_two = shift(own, 2)
    high_two = shift(own, -2)
    struct_rows = lax.all_to_all(rows, "struct", 0, 0, tiled=True).reshape(2 * DEVS, LANES)

    mine = 2 * lax.axis_index("fluid")
    take = lambda a, axis: lax.dynamic_slice_in_dim(a, mine, 2, axis)
    blocks = take(shell_blocks, 1).reshape(NB, 2, BLK, BLK)
    inverse = take(shell_inverse, 0).reshape(2, BLK, BLK)
    columns = take(shell_columns, 1)
    rhs_rows = take(struct_rhs.reshape(2 * FLUID, BLK), 0)

    packs = [own, low_two, high_two, low, high, shift(low[1], 2), shift(high[0], -2)]
    relay = ((lax.axis_index(BOTH)) // CHUNKS).astype(jnp.int32).reshape(1)

    def shell(struct_rows, start):
        (terms,) = call(
            functools.partial(shell_kernel, start), "shell", [(2, BLK)], [VMEM, VMEM, SMEM]
        )(struct_rows, blocks, columns)
        return terms

    def solve(shares, terms, shape, scratch, held=()):
        received = lax.all_to_all(shares, BOTH, 0, 0, tiled=True)
        (solved,) = call(
            functools.partial(solve_kernel, len(held)), "solve", [shape],
            [VMEM] * 4 + [SMEM] + [VMEM] * len(held), scratch,
        )(received, rhs_rows, terms, inverse, relay, *held)
        return solved

    terms = shell(struct_rows, True)
    state, shares = fluid(True, packs, struct_rows)
    solved = solve(shares, terms, (4 * DEVS, LANES), [pltpu.VMEM((DEVS + 16, LANES), f32)],
                   packs[5:])
    struct_rows = lax.all_to_all(solved, BOTH, 0, 0, tiled=True)
    terms = shell(struct_rows, False)
    state, shares = fluid(False, packs, struct_rows, state)
    solved = solve(shares, terms, (2 * FLUID, LANES), [])
    group = lax.all_to_all(solved, "fluid", 0, 0, tiled=True)
    return (state, group[:, 0:BLK].reshape(-1))


def solution(mesh):
    placed = (
        P(None, ("fluid", "struct")),
        P(None, ("fluid", "struct")),
        P(None, None, ("fluid", "struct")),
        P(None, None, None, ("fluid", "struct")),
        P(None, ("fluid", "struct")),
        P(("fluid", "struct")),
        P(("fluid", "struct")),
        P(None, ("fluid", "struct")),
        P(None, ("fluid", "struct")),
        P(None, None, ("fluid", "struct")),
        P(None, None, ("fluid", "struct")),
        P("struct"),
        P("struct"),
        P(None, "struct", None),
        P("struct", None),
        P(None, "struct"),
    )
    return jax.shard_map(
        body,
        mesh=mesh,
        in_specs=placed,
        out_specs=(P(None, ("fluid", "struct")), P("struct")),
        check_vma=False,
    )
```
